32 devices in a mesh: shot: 8 (over z, y), rcv: 4 (over x, core).
Axes of the slice: x: 2, y: 2, z: 4, core: 2. Of those that a mesh axis runs over, the one named last changes fastest.
Arguments:
- record: bfloat16 [8192, 2048], P('shot', 'rcv'), may hold values from -6 to 6
- offsets: int32 [8], P('shot'), may hold values from 0 to 1023
- lengths: int32 [8], P('shot'), may hold values from 1024 to 2048
- thresholds: float32 [3], replicated, may hold values from 0.05 to 0.5
Outputs:
- estimate: float32 [8, 2048, 2048], P('shot', None, 'rcv')
The draws below stay inside these ranges and needn't reach their ends.
All inputs are finite; a program needn't handle non-finite values.
Results may differ from the reference program's by a relative error of at most 0.0003.
Values sent between devices are 32-bit elements; how exact they have to be, the bound alone decides.
No kernel may reach another device: no remote copies, remote signals or barrier semaphores. Data moves between devices by JAX's collectives and lax.ppermute only.
A program may use at most 64 MiB of HBM per device.

```python
import math
import jax
import jax.numpy as jnp
from jax import lax

NT = 2048
NREC = 2048
LEVELS = 3
ITERS = 2
SEG = 1024
SHOTS = 8
TT = 8192


def plant(result, stream_key, smallest, high):
    place = [jax.random.randint(jax.random.fold_in(stream_key, axis), (), 0, length) for axis, length in enumerate(result.shape)]
    main_axis = result.shape.index(max(result.shape))
    beside = place[:main_axis] + [(place[main_axis] + 1) % result.shape[main_axis]] + place[main_axis + 1:]
    return result.at[tuple(place)].set(smallest).at[tuple(beside)].set(high)


def steps_of(rng, shape, cuts, smallest, largest):
    def one(dim, blocks):
        draws = jax.random.uniform(jax.random.fold_in(jax.random.fold_in(rng, 6), dim), (blocks,), jnp.float32, smallest / len(cuts), largest / len(cuts))
        return jnp.repeat(jnp.exp(draws), shape[dim] // blocks).reshape((-1,) + (1,) * (len(shape) - dim - 1))

    loudness = one(*cuts[0])
    for cut in cuts[1:]:
        loudness = loudness * one(*cut)
    return loudness


def noise(rng, shape, scale, reach, shards=(), kind=jnp.bfloat16):
    values = jax.random.normal(rng, shape, jnp.float32) * scale
    if len(shards) > 0:
        values = steps_of(rng, shape, shards, -0.22, 0.18) * values
    return jnp.clip(values, min=-reach, max=reach).astype(kind)


def setup_inputs(seed: int = 0) -> dict:
    key_of = jax.random.split(jax.random.key(seed), 5)
    return {
        "record": noise(key_of[0], (TT, NREC), 1.0, 6.0, ((0, 8), (1, 4))),
        "offsets": plant(jax.random.randint(key_of[1], (SHOTS,), 0, SEG), jax.random.fold_in(key_of[1], 1), 0, SEG - 1).astype(jnp.int32),
        "lengths": plant(jax.random.randint(key_of[2], (SHOTS,), NT // 2, NT + 1), jax.random.fold_in(key_of[2], 1), NT // 2, NT).astype(jnp.int32),
        "thresholds": jnp.clip(jnp.exp(jax.random.uniform(key_of[3], (LEVELS,), jnp.float32, math.log(0.05), math.log(0.5))), 0.05, 0.5),
    }


SPLINE_TAPS = (0.0625, 0.25, 0.375, 0.25, 0.0625)
relax_step = 0.5


def smooth_time(signal, dilation):
    length_rows = signal.shape[0]
    padded = jnp.pad(signal, ((2 * dilation, 2 * dilation), (0, 0)))
    summed = SPLINE_TAPS[0] * padded[0:length_rows]
    for tap_index in range(1, 5):
        summed = summed + SPLINE_TAPS[tap_index] * padded[tap_index * dilation:tap_index * dilation + length_rows]
    return summed


def smooth_across(signal, dilation):
    columns = signal.shape[1]
    padded = jnp.pad(signal, ((0, 0), (2 * dilation, 2 * dilation)))
    summed = SPLINE_TAPS[0] * padded[:, 0:columns]
    for tap_index in range(1, 5):
        summed = summed + SPLINE_TAPS[tap_index] * padded[:, tap_index * dilation:tap_index * dilation + columns]
    return summed


def soft_limit(values, level_cut):
    return values - jnp.clip(values, -level_cut, level_cut)


def shrink(signal, thresholds):
    current = signal
    shrunk = jnp.zeros_like(signal)
    for level_index in range(LEVELS):
        dilation = 2 ** level_index
        coarser = smooth_across(smooth_time(current, dilation), dilation)
        shrunk = shrunk + soft_limit(current - coarser, thresholds[level_index])
        current = coarser
    return shrunk + current


def reference(record, offsets, lengths, thresholds):
    measured = record.astype(jnp.float32)
    anchors = jnp.arange(SHOTS, dtype=jnp.int32) * SEG + offsets
    time_index = jnp.arange(NT, dtype=jnp.int32)
    live_mask = (time_index[None, :] < lengths[:, None]).astype(jnp.float32)
    estimate = jnp.zeros((SHOTS, NT, NREC), jnp.float32)
    zero_tail = jnp.zeros((2 * SEG, NREC), jnp.float32)
    for sweep_index in range(ITERS):
        if sweep_index == 0:
            misfit = measured
        else:
            def spread(shot_index, predicted):
                anchor = anchors[shot_index]
                current = lax.dynamic_slice(predicted, (anchor, jnp.int32(0)), (NT, NREC))
                return lax.dynamic_update_slice(predicted, current + estimate[shot_index], (anchor, jnp.int32(0)))

            predicted = lax.fori_loop(0, SHOTS, spread, jnp.zeros((SHOTS * SEG + 2 * SEG, NREC), jnp.float32))
            misfit = measured - predicted[:SHOTS * SEG]
        extended = jnp.concatenate([misfit, zero_tail], axis=0)

        def update(shot_items):
            current, anchor, mask_row = shot_items
            windowed = lax.dynamic_slice(extended, (anchor, jnp.int32(0)), (NT, NREC))
            gathered = current + relax_step * mask_row[:, None] * windowed
            return mask_row[:, None] * shrink(gathered, thresholds)

        estimate = lax.map(update, (estimate, anchors, live_mask))
    return estimate
```

```python
import numpy as np
import jax
import jax.numpy as jnp
from jax import lax
from jax.experimental import pallas as pl
from jax.experimental.pallas import tpu as pltpu
from jax.sharding import PartitionSpec as P

LEVELS = 3
relax_step = 0.5

PLANES = 5
LANES = 128
RING = PLANES * LANES
EDGE = 32
PAD = 64
ROWHALO = 16
BLOCK = 32


def shifted(shard, axis, by):
    devices = lax.axis_size(axis)
    pairs = [(i, i + by) for i in range(devices) if 0 <= i + by < devices]
    return lax.ppermute(shard, axis, pairs)


def ring_matrices(columns):
    wide = columns + 2 * LANES
    into = np.zeros((wide, RING), np.float32)
    back = np.zeros((RING, columns), np.float32)

    def place(ring):
        return (ring % PLANES) * LANES + ring // PLANES

    for column in range(columns):
        into[column, place(column)] = relax_step
        back[place(column), column] = 1.0
    for quarter in range(LANES // EDGE):
        for i in range(EDGE):
            into[columns + quarter * EDGE + i, place(RING - EDGE + i)] = relax_step
            into[columns + LANES + quarter * EDGE + i, place(columns + i)] = relax_step
    return jnp.asarray(into, jnp.bfloat16), jnp.asarray(back, jnp.bfloat16)


def ring_shift(planes, by):
    out = []
    for k in range(PLANES):
        turns, plane = divmod(k + by, PLANES)
        value = planes[plane]
        if turns:
            value = pltpu.roll(value, (-turns) % LANES, 1)
        out.append(value)
    return out


def add_all(a, b):
    return [x + y for x, y in zip(a, b)]


def smooth_across(planes, dilation):
    for _ in range(2):
        planes = add_all(planes, ring_shift(planes, dilation))
        planes = add_all(planes, ring_shift(planes, -dilation))
    return planes


def smooth_block(ref, start, rows, dilation, scale):
    centre, summed = [], []
    for k in range(PLANES):
        x = [ref[k, pl.ds(start + tap * dilation, rows), :] for tap in range(-2, 3)]
        centre.append(x[2])
        summed.append((x[0] + x[4]) + 4.0 * (x[1] + x[3]) + 6.0 * x[2])
    summed = smooth_across(summed, dilation)
    return centre, [s * w for s, w in zip(summed, scale)]


def limit(values, cut):
    return jnp.minimum(jnp.maximum(values, -cut), cut)


def deblend_kernel(
    scal, thr, own, own_h, near, near_h, far, far_h, top, bot, into, back,
    out, ext, g, c1, c2, f, g2, strip, sem,
):
    seg = own.shape[0]
    columns = own.shape[1]
    window = 2 * seg
    tiles = columns // LANES
    quarter = seg // (LANES // EDGE)
    copies = []

    def bring(src, dst):
        copy = pltpu.make_async_copy(src, dst, sem.at[len(copies)])
        copy.start()
        copies.append(copy)

    for j in range(tiles + 2):
        lanes = pl.ds(j * LANES, LANES)
        bring(top.at[:, lanes], ext.at[j, pl.ds(0, ROWHALO), :])
        bring(bot.at[:, lanes], ext.at[j, pl.ds(ROWHALO + 3 * seg, ROWHALO), :])
    for n, (main, halo) in enumerate(((own, own_h), (near, near_h), (far, far_h))):
        base = ROWHALO + n * seg
        for j in range(tiles):
            bring(main.at[:, pl.ds(j * LANES, LANES)], ext.at[j, pl.ds(base, seg), :])
        for side in range(2):
            for q in range(LANES // EDGE):
                bring(
                    halo.at[pl.ds(side * quarter, quarter), :],
                    ext.at[tiles + side, pl.ds(base + q * quarter, quarter), :],
                )

    offset = scal[0]
    live = scal[8]
    total = scal[11]
    lane = lax.broadcasted_iota(jnp.int32, (1, LANES), 1)
    scale = []
    for k in range(PLANES):
        ring = lane * PLANES + k
        right = jnp.where(scal[13] > 0, 1.0, 0.0)
        left = jnp.where(scal[12] > 0, 1.0, 0.0)
        middle = columns + LANES // 2
        valid = jnp.where(ring < columns, 1.0, jnp.where(ring < middle, right, left))
        scale.append(valid * (1.0 / 256.0))

    zeros = jnp.zeros((PLANES, PAD, LANES), jnp.float32)
    g[:, 0:PAD, :] = zeros
    g[:, PAD + window : 2 * PAD + window, :] = zeros
    for ref in (g2, c1, c2):
        ref[:, 0:PAD, :] = zeros
        ref[:, PAD + window : 2 * PAD + window, :] = zeros
    for copy in copies:
        copy.wait()

    span = window + 2 * ROWHALO
    mm = span // 10

    def permute_in(b, carry):
        start = offset + b * mm
        row = start - ROWHALO + lax.broadcasted_iota(jnp.int32, (mm, 1), 0)
        part = lax.shift_right_arithmetic(row, quarter.bit_length() - 1) & (LANES // EDGE - 1)
        mine = (lane // EDGE) == part
        pieces = [ext[j, pl.ds(start, mm), :] for j in range(tiles)]
        for side in range(2):
            pieces.append(jnp.where(mine, ext[tiles + side, pl.ds(start, mm), :], 0.0))
        lhs = jnp.concatenate([p.astype(jnp.bfloat16) for p in pieces], axis=1)
        result = jnp.dot(lhs, into[...], preferred_element_type=jnp.float32)
        at = pl.multiple_of(PAD - ROWHALO + b * mm, 8)
        for k in range(PLANES):
            g[k, pl.ds(at, mm), :] = result[:, k * LANES : (k + 1) * LANES]
        return carry

    lax.fori_loop(0, 10, permute_in, 0)

    def level_pass(source, target, dilation, first, blocks):
        def body(b, carry):
            at = pl.multiple_of(first + b * BLOCK, 8)
            _, summed = smooth_block(source, at, BLOCK, dilation, scale)
            for k in range(PLANES):
                target[k, pl.ds(at, BLOCK), :] = summed[k]
            return carry

        lax.fori_loop(0, blocks, body, 0)

    def last_pass(base_ref, at, rows):
        centre, summed = smooth_block(c2, at, rows, 4, scale)
        result = []
        for k in range(PLANES):
            x0 = base_ref[k, pl.ds(at, rows), :]
            x1 = c1[k, pl.ds(at, rows), :]
            x2 = centre[k]
            clipped = limit(x0 - x1, thr[0]) + limit(x1 - x2, thr[1]) + limit(x2 - summed[k], thr[2])
            result.append((x0, x0 - clipped))
        return result

    level_pass(g, c1, 1, PAD - ROWHALO, (window + 2 * ROWHALO) // BLOCK)
    level_pass(c1, c2, 2, PAD - ROWHALO, (window + 2 * ROWHALO) // BLOCK)

    def row_factor(t):
        count = jnp.zeros(t.shape, jnp.float32)
        for n in range(5):
            begin, length = scal[1 + n], scal[6 + n]
            count = count + jnp.where((t >= begin) & (t < begin + length), 1.0, 0.0)
        own_live = jnp.where(t < live, 1.0, 0.0)
        inside = jnp.where(t < total, relax_step, 0.0)
        return own_live, own_live * (1.0 - inside * count)

    def f_pass(b, carry):
        at = pl.multiple_of(PAD + b * BLOCK, 8)
        t = b * BLOCK + lax.broadcasted_iota(jnp.int32, (BLOCK, LANES), 0)
        own_live, factor = row_factor(t)
        for k, (x0, value) in enumerate(last_pass(g, at, BLOCK)):
            f[k, pl.ds(at, BLOCK), :] = value
            g2[k, pl.ds(at, BLOCK), :] = own_live * x0 + factor * value
        return carry

    lax.fori_loop(0, window // BLOCK, f_pass, 0)

    half = 32
    rows = 2 * half

    def do_strip(begin, length, at_end, is_own):
        p = begin + (length if at_end else 0)
        t = p - half + lax.broadcasted_iota(jnp.int32, (rows, LANES), 0)
        in_live = jnp.where((t >= begin) & (t < begin + length), 1.0, 0.0)
        in_window = jnp.where((t >= begin) & (t < begin + window), 1.0, 0.0)
        for k in range(PLANES):
            strip[0, k, 16 : 16 + rows, :] = g[k, pl.ds(PAD + p - half, rows), :] * in_live
        for j in range(2):
            _, summed = smooth_block(strip.at[j], 16, rows, 2**j, scale)
            for k in range(PLANES):
                strip[j + 1, k, 16 : 16 + rows, :] = summed[k] * in_window
        mid = 16 + half - 16
        _, summed = smooth_block(strip.at[2], mid, 32, 4, scale)
        t = p - 16 + lax.broadcasted_iota(jnp.int32, (32, LANES), 0)
        shot_live = jnp.where((t >= begin) & (t < begin + length), 1.0, 0.0)
        near_edge = jnp.where((t >= p - 14) & (t < p + 14), shot_live, 0.0)
        own_live = jnp.where((t >= 0) & (t < live), near_edge, 0.0)
        inside = jnp.where(t < total, -relax_step, 0.0)
        weight = own_live * (inside + (1.0 if is_own else 0.0))
        in_window = jnp.where((t >= begin) & (t < begin + window), 1.0, 0.0)
        for k in range(PLANES):
            x0 = strip[0, k, mid : mid + 32, :]
            x1 = strip[1, k, mid : mid + 32, :]
            x2 = strip[2, k, mid : mid + 32, :]
            x3 = summed[k] * in_window
            clipped = limit(x0 - x1, thr[0]) + limit(x1 - x2, thr[1]) + limit(x2 - x3, thr[2])
            where = pl.ds(PAD + p - 16, 32)
            g2[k, where, :] = g2[k, where, :] + weight * (x0 - clipped - f[k, where, :])

    f[:, 0:PAD, :] = zeros
    f[:, PAD + window : 2 * PAD + window, :] = zeros
    strip[:, :, 0:16, :] = jnp.zeros((3, PLANES, 16, LANES), jnp.float32)
    strip[:, :, 16 + rows : 32 + rows, :] = jnp.zeros((3, PLANES, 16, LANES), jnp.float32)
    for n in range(5):
        for at_end in (False, True):
            if n == 0 and not at_end:
                continue
            begin, length = scal[1 + n], scal[6 + n]
            p = begin + (length if at_end else 0)
            low, high = (p - 14, p) if at_end else (p, p + 14)

            @pl.when((length > 0) & (high > 0) & (low < live))
            def _():
                do_strip(begin, length, at_end, n == 2)

    for ref in (c1, c2):
        ref[:, PAD - ROWHALO : PAD, :] = jnp.zeros((PLANES, ROWHALO, LANES), jnp.float32)
        ref[:, PAD + window : PAD + window + ROWHALO, :] = jnp.zeros((PLANES, ROWHALO, LANES), jnp.float32)
    level_pass(g2, c1, 1, PAD, window // BLOCK)
    level_pass(c1, c2, 2, PAD, window // BLOCK)

    def e_pass(b, carry):
        at = pl.multiple_of(PAD + b * BLOCK, 8)
        t = b * BLOCK + lax.broadcasted_iota(jnp.int32, (BLOCK, LANES), 0)
        own_live = jnp.where(t < live, 1.0, 0.0)
        for k, (_, value) in enumerate(last_pass(g2, at, BLOCK)):
            f[k, pl.ds(at, BLOCK), :] = own_live * value
        return carry

    lax.fori_loop(0, window // BLOCK, e_pass, 0)

    mo = 256

    def permute_out(b, carry):
        at = pl.multiple_of(PAD + b * mo, 8)
        high, low = [], []
        for k in range(PLANES):
            x = f[k, pl.ds(at, mo), :]
            h = x.astype(jnp.bfloat16)
            high.append(h)
            low.append((x - h.astype(jnp.float32)).astype(jnp.bfloat16))
        matrix = back[...]
        result = jnp.dot(jnp.concatenate(high, axis=1), matrix, preferred_element_type=jnp.float32)
        result = result + jnp.dot(jnp.concatenate(low, axis=1), matrix, preferred_element_type=jnp.float32)
        out[0, pl.ds(pl.multiple_of(b * mo, 8), mo), :] = result
        return carry

    lax.fori_loop(0, window // mo, permute_out, 0)


def on_device(record, offsets, lengths, thresholds):
    seg, columns = record.shape
    window = 2 * seg
    shots = lax.axis_size("shot")
    rcvs = lax.axis_size("rcv")
    me = lax.axis_index("shot")
    rcv = lax.axis_index("rcv")
    odd = me % 2 == 1
    main = record.astype(jnp.float32)

    quarters = LANES // EDGE

    def pack(edge):
        return edge.reshape(quarters, seg // quarters, EDGE).transpose(1, 0, 2).reshape(seg // quarters, LANES)

    from_left = shifted(pack(main[:, columns - EDGE :]), "rcv", 1)
    from_right = shifted(pack(main[:, :EDGE]), "rcv", -1)
    halo = jnp.concatenate([from_left, from_right], axis=0)

    quarter = seg // quarters
    wide_first = jnp.concatenate([main[:ROWHALO], from_left[:ROWHALO], from_right[:ROWHALO]], axis=1)
    wide_last = jnp.concatenate(
        [main[-ROWHALO:], from_left[quarter - ROWHALO :], from_right[quarter - ROWHALO :]], axis=1
    )
    top = shifted(wide_last, "shot", 1)
    bot = shifted(wide_first, "shot", -3)

    far = shifted(main, "shot", -2)
    far_h = shifted(halo, "shot", -2)
    swap = [(i, i ^ 1) for i in range(shots) if i ^ 1 < shots]
    near = lax.ppermute(jnp.where(odd, main, far), "shot", swap)
    near_h = lax.ppermute(jnp.where(odd, halo, far_h), "shot", swap)

    mine = jnp.stack([offsets[0], lengths[0]])
    pairs = [shifted(mine, "shot", -by) if by else mine for by in range(-2, 3)]
    begins = [by * seg + pair[0] - offsets[0] for by, pair in zip(range(-2, 3), pairs)]
    total = shots * seg - me * seg - offsets[0]
    scal = jnp.stack(
        [offsets[0]] + begins + [pair[1] for pair in pairs]
        + [total, (rcv > 0).astype(jnp.int32), (rcv < rcvs - 1).astype(jnp.int32)]
    )
    into, back = ring_matrices(columns)
    deep = window + 2 * PAD
    work = pltpu.VMEM((PLANES, deep, LANES), jnp.float32)
    smem = pl.BlockSpec(memory_space=pltpu.SMEM)
    anywhere = pl.BlockSpec(memory_space=pl.ANY)
    vmem = pl.BlockSpec(memory_space=pltpu.VMEM)
    return pl.pallas_call(
        deblend_kernel,
        out_shape=jax.ShapeDtypeStruct((1, window, columns), jnp.float32),
        in_specs=[smem, smem] + [anywhere] * 8 + [vmem, vmem],
        out_specs=vmem,
        scratch_shapes=[
            pltpu.VMEM((columns // LANES + 2, 3 * seg + 2 * ROWHALO, LANES), jnp.float32),
            work, work, work, work, work,
            pltpu.VMEM((3, PLANES, 96, LANES), jnp.float32),
            pltpu.SemaphoreType.DMA((64,)),
        ],
        compiler_params=pltpu.CompilerParams(vmem_limit_bytes=60 * 1024 * 1024),
    )(scal, thresholds, main, halo, near, near_h, far, far_h, top, bot, into, back)


def solution(mesh):
    return jax.shard_map(
        on_device,
        mesh=mesh,
        in_specs=(P("shot", "rcv"), P("shot"), P("shot"), P()),
        out_specs=P("shot", None, "rcv"),
        check_vma=False,
    )
```

```python
import functools

import numpy as np
import jax
import jax.numpy as jnp
from jax import lax
from jax.experimental import pallas as pl
from jax.experimental.pallas import tpu as pltpu
from jax.sharding import PartitionSpec as P

LEVELS = 3
relax_step = 0.5

PLANES = 5
LANES = 128
RING = PLANES * LANES
EDGE = 32
QUARTERS = LANES // EDGE
HEAD = 128
PAD = 64
ROWHALO = 16
BLOCK = 64
STRIP = 64


def shifted(shard, axis, by):
    devices = lax.axis_size(axis)
    pairs = [(i, i + by) for i in range(devices) if 0 <= i + by < devices]
    return lax.ppermute(shard, axis, pairs)


def ring_matrices(columns):
    wide = columns + 2 * LANES
    into = np.zeros((wide, RING), np.float32)
    back = np.zeros((RING, columns), np.float32)

    def place(ring):
        return (ring % PLANES) * LANES + ring // PLANES

    for column in range(columns):
        into[column, place(column)] = relax_step
        back[place(column), column] = 1.0
    for quarter in range(LANES // EDGE):
        for i in range(EDGE):
            into[columns + quarter * EDGE + i, place(RING - EDGE + i)] = relax_step
            into[columns + LANES + quarter * EDGE + i, place(columns + i)] = relax_step
    return jnp.asarray(into, jnp.bfloat16), jnp.asarray(back, jnp.bfloat16)


def smooth_across(planes, dilation):
    rolled = {}

    def at(position):
        turns, plane = divmod(position, PLANES)
        if turns == 0:
            return planes[plane]
        if (turns, plane) not in rolled:
            rolled[turns, plane] = pltpu.roll(planes[plane], (-turns) % LANES, 1)
        return rolled[turns, plane]

    return [
        (at(k - 2 * dilation) + at(k + 2 * dilation))
        + 4.0 * (at(k - dilation) + at(k + dilation))
        + 6.0 * planes[k]
        for k in range(PLANES)
    ]


def limit(values, cut):
    return jnp.minimum(jnp.maximum(values, -cut), cut)


def blocks_of(first, count, body):
    def step(b, carry):
        at = pl.multiple_of(first + b * (2 * BLOCK), 8)
        body(at, BLOCK)
        body(pl.multiple_of(at + BLOCK, 8), BLOCK)
        return carry

    lax.fori_loop(0, count // 2, step, 0)

    @pl.when(count % 2 == 1)
    def _():
        body(pl.multiple_of(first + (count - 1) * BLOCK, 8), BLOCK)


def smooth_block(ref, start, rows, dilation, scale):
    centre, summed = [], []
    for k in range(PLANES):
        x = [ref[k, pl.ds(start + tap * dilation, rows), :] for tap in range(-2, 3)]
        centre.append(x[2])
        summed.append((x[0] + x[4]) + 4.0 * (x[1] + x[3]) + 6.0 * x[2])
    summed = smooth_across(summed, dilation)
    return centre, [s * w for s, w in zip(summed, scale)]


def deblend_kernel(geometry, pieces, span, aliased, params, thr, into, back, *refs):
    seg, columns, arrays = geometry
    refs = refs[:arrays] + refs[arrays + aliased :]
    sources = refs[:arrays]
    out, g, c1, c2, f, g2, strip, staged, sem = refs[arrays:]
    window = 2 * seg
    quarter_rows = seg // QUARTERS

    shots = lax.axis_size("shot")
    me = lax.axis_index("shot")
    rcv = lax.axis_index("rcv")
    offset = params[2, 0]
    live = params[2, 1]
    total = (shots - me) * seg - offset

    def shot(by):
        return by * seg + params[by + 2, 0] - offset, params[by + 2, 1]

    low, count = span(offset)
    low = pl.multiple_of(low, 8)
    high = low + count * BLOCK

    lane = lax.broadcasted_iota(jnp.int32, (1, LANES), 1)
    has_right = jnp.where(rcv < lax.axis_size("rcv") - 1, 1.0, 0.0)
    has_left = jnp.where(rcv > 0, 1.0, 0.0)
    scale = []
    for k in range(PLANES):
        ring = lane * PLANES + k
        side = jnp.where(ring < columns + LANES // 2, has_right, has_left)
        scale.append(jnp.where(ring < columns, 1.0, side) * (1.0 / 256.0))

    def permute_in(main, halo, first, rows, quarter, row):
        lhs = [sources[main][pl.ds(first, rows), 0:columns].astype(jnp.bfloat16)]
        mine = (lane // EDGE) == quarter
        for side in range(2):
            if halo is None:
                part = sources[main][0:rows, columns + side * LANES : columns + (side + 1) * LANES]
            else:
                inner, part = row % quarter_rows, []
                while inner < row % quarter_rows + rows:
                    at = (2 * side + inner // HEAD) * LANES
                    end = min(inner // HEAD * HEAD + HEAD, row % quarter_rows + rows)
                    part.append(sources[halo][inner % HEAD : inner % HEAD + end - inner, at : at + LANES])
                    inner = end
                part = jnp.concatenate(part, axis=0)
            lhs.append(jnp.where(mine, part, 0.0).astype(jnp.bfloat16))
        result = jnp.dot(jnp.concatenate(lhs, axis=1), into[...], preferred_element_type=jnp.float32)
        for k in range(PLANES):
            g[k, PAD + row : PAD + row + rows, :] = result[:, k * LANES : (k + 1) * LANES]

    for parity, *piece in pieces:
        rows, row = piece[3], piece[5]
        wanted = (count > 0) & (row < offset + high + 40) & (row + rows > offset + low - 40)
        if parity is not None:
            wanted = wanted & (lax.rem(me, 2) == parity)

        @pl.when(wanted)
        def _():
            permute_in(*piece)

    def level_pass(source, shift, target, dilation, first, count):
        def body(at, rows):
            _, summed = smooth_block(source, at + shift, rows, dilation, scale)
            for k in range(PLANES):
                target[k, pl.ds(at, rows), :] = summed[k]

        blocks_of(first, count, body)

    def last_pass(base_ref, shift, at, rows):
        centre, summed = smooth_block(c2, at, rows, 4, scale)
        for k in range(PLANES):
            x0 = base_ref[k, pl.ds(at + shift, rows), :]
            x1 = c1[k, pl.ds(at, rows), :]
            x2 = centre[k]
            clipped = limit(x0 - x1, thr[0]) + limit(x1 - x2, thr[1]) + limit(x2 - summed[k], thr[2])
            yield k, x0, x0 - clipped

    def f_pass(at, rows):
        t = at - PAD + lax.broadcasted_iota(jnp.int32, (rows, LANES), 0)
        count = jnp.zeros(t.shape, jnp.float32)
        for by in range(-2, 3):
            begin, length = shot(by)
            count = count + jnp.where((t >= begin) & (t < begin + length), 1.0, 0.0)
        own_live = jnp.where((t >= 0) & (t < live), 1.0, 0.0)
        inside = jnp.where(t < total, relax_step, 0.0)
        factor = own_live * (1.0 - inside * count)
        for k, x0, value in last_pass(g, offset, at, rows):
            f[k, pl.ds(at, rows), :] = value
            g2[k, pl.ds(at, rows), :] = own_live * x0 + factor * value

    half = STRIP // 2

    def do_strip(by, at_end):
        begin, length = shot(by)
        p = begin + jnp.where(at_end, length, 0)
        t = p - half + lax.broadcasted_iota(jnp.int32, (STRIP, LANES), 0)
        in_live = jnp.where((t >= begin) & (t < begin + length), 1.0, 0.0)
        in_window = jnp.where((t >= begin) & (t < begin + window), 1.0, 0.0)
        for k in range(PLANES):
            strip[0, k, 16 : 16 + STRIP, :] = g[k, pl.ds(PAD + offset + p - half, STRIP), :] * in_live
        for j in range(2):
            _, summed = smooth_block(strip.at[j], 16, STRIP, 2**j, scale)
            for k in range(PLANES):
                strip[j + 1, k, 16 : 16 + STRIP, :] = summed[k] * in_window
        mid = half
        _, summed = smooth_block(strip.at[2], mid, 32, 4, scale)
        t = p - 16 + lax.broadcasted_iota(jnp.int32, (32, LANES), 0)
        in_window = jnp.where((t >= begin) & (t < begin + window), 1.0, 0.0)
        near_edge = (t >= begin) & (t < begin + length) & (t >= p - 14) & (t < p + 14)
        own_live = (t >= 0) & (t < live)
        inside = jnp.where(t < total, -relax_step, 0.0)
        weight = jnp.where(near_edge & own_live, inside + jnp.where(by == 0, 1.0, 0.0), 0.0)
        for k in range(PLANES):
            x0 = strip[0, k, mid : mid + 32, :]
            x1 = strip[1, k, mid : mid + 32, :]
            x2 = strip[2, k, mid : mid + 32, :]
            x3 = summed[k] * in_window
            clipped = limit(x0 - x1, thr[0]) + limit(x1 - x2, thr[1]) + limit(x2 - x3, thr[2])
            where = pl.ds(PAD + p - 16, 32)
            g2[k, where, :] = g2[k, where, :] + weight * (x0 - clipped - f[k, where, :])

    def e_pass(at, rows):
        t = at - PAD + lax.broadcasted_iota(jnp.int32, (rows, LANES), 0)
        own_live = jnp.where(t < live, 1.0, 0.0)
        for k, _, value in last_pass(g2, 0, at, rows):
            f[k, pl.ds(at, rows), :] = own_live * value

    def permute_out(at, rows):
        high, low = [], []
        for k in range(PLANES):
            x = f[k, pl.ds(at, rows), :]
            h = x.astype(jnp.bfloat16)
            high.append(h)
            low.append((x - h.astype(jnp.float32)).astype(jnp.bfloat16))
        both = jnp.concatenate([jnp.concatenate(high, axis=1), jnp.concatenate(low, axis=1)], axis=0)
        result = jnp.dot(both, back[...], preferred_element_type=jnp.float32)
        staged[pl.ds(pl.multiple_of(at - PAD, 8), rows), :] = result[:rows] + result[rows:]

    def clear_edges(ref):
        ref[:, PAD - 16 : PAD, :] = jnp.zeros((PLANES, 16, LANES), jnp.float32)
        ref[:, PAD + window : PAD + window + 16, :] = jnp.zeros((PLANES, 16, LANES), jnp.float32)

    strip[:, :, 0:16, :] = jnp.zeros((3, PLANES, 16, LANES), jnp.float32)
    strip[:, :, 16 + STRIP : 32 + STRIP, :] = jnp.zeros((3, PLANES, 16, LANES), jnp.float32)

    def process():
        first = PAD + low
        outer, many = first - BLOCK // 2, count + 1
        level_pass(g, offset, c1, 1, outer, many)
        level_pass(c1, 0, c2, 2, outer, many)
        blocks_of(outer, many, f_pass)

        def strip_step(i, carry):
            by, at_end = i // 2 - 2, i % 2 == 1
            begin, length = shot(by)
            p = begin + jnp.where(at_end, length, 0)
            begins_at = jnp.where(at_end, p - 14, p)
            bottom = jnp.maximum(low - 14, 0)
            top = jnp.minimum(high + 14, live)

            @pl.when((length > 0) & (begins_at + 14 > bottom) & (begins_at < top))
            def _():
                do_strip(by, at_end)

            return carry

        lax.fori_loop(1, 10, strip_step, 0)
        clear_edges(g2)
        level_pass(g2, 0, c1, 1, outer, many)
        clear_edges(c1)
        level_pass(c1, 0, c2, 2, outer, many)
        clear_edges(c2)
        blocks_of(first, count, e_pass)
        blocks_of(first, count, permute_out)

        def copy(i):
            rows = pl.ds(pl.multiple_of(low + i * BLOCK, 8), BLOCK)
            return pltpu.make_async_copy(staged.at[rows, :], out.at[0, rows, :], sem.at[i])

        def start(i, carry):
            copy(i).start()
            return carry

        def wait(i, carry):
            copy(i).wait()
            return carry

        lax.fori_loop(0, count, start, 0)
        lax.fori_loop(0, count, wait, 0)

    @pl.when(count > 0)
    def _():
        process()


def prepare_kernel(record, first_edge, last_edge):
    seg, columns = record.shape
    quarter = seg // QUARTERS
    lane = lax.broadcasted_iota(jnp.int32, (1, LANES), 1)
    for out, start, inner in ((first_edge, 0, 0), (last_edge, columns - LANES, LANES - EDGE)):
        packed = jnp.zeros((quarter, LANES), jnp.float32)
        for q in range(QUARTERS):
            rows = record[q * quarter : (q + 1) * quarter, start : start + LANES].astype(jnp.float32)
            turn = (q * EDGE - inner) % LANES
            packed = jnp.where(lane // EDGE == q, pltpu.roll(rows, turn, 1) if turn else rows, packed)
        out[...] = packed


def header_kernel(parts, offsets, lengths, record, left, right, wide_first, wide_last, *own):
    seg, columns = record.shape
    quarter = seg // QUARTERS
    lane = lax.broadcasted_iota(jnp.int32, (8, LANES), 1)
    about = jnp.where(lane == 0, offsets[0], jnp.where(lane == 1, lengths[0], 0)).astype(jnp.float32)
    first = own[0]
    for side, halo in enumerate((left, right)):
        for part in range(quarter // HEAD):
            at = (2 * side + part) * LANES
            first[0:HEAD, at : at + LANES] = halo[part * HEAD : (part + 1) * HEAD, :]
    first[HEAD : HEAD + 8, :] = jnp.concatenate([about] * (columns // LANES), axis=1)
    first[HEAD + 8 :, :] = record[0 : parts[1], :].astype(jnp.float32)
    for k in range(1, len(own)):
        own[k][...] = record[parts[k] : parts[k + 1], :].astype(jnp.float32)
    wide_first[:, 0:columns] = record[0:ROWHALO, :].astype(jnp.float32)
    wide_last[0:ROWHALO, 0:columns] = record[seg - ROWHALO : seg, :].astype(jnp.float32)
    for side, halo in enumerate((left, right)):
        at = columns + side * LANES
        wide_first[:, at : at + LANES] = halo[0:ROWHALO, :]
        wide_last[0:ROWHALO, at : at + LANES] = halo[quarter - ROWHALO : quarter, :]
    wide_last[ROWHALO:, :] = jnp.concatenate([about] * (columns // LANES + 2), axis=1)


def on_device(record, offsets, lengths, thresholds):
    seg, columns = record.shape
    window = 2 * seg
    shots = lax.axis_size("shot")
    q = seg // QUARTERS
    skip = HEAD + 8
    step = (seg + skip + 4 * 16 - 1) // (4 * 16) * 16
    parts = [0] + [seg - k * step for k in (3, 2, 1, 0)]
    swap = [(i, i ^ 1) for i in range(shots) if i ^ 1 < shots]
    smem = pl.BlockSpec(memory_space=pltpu.SMEM)
    anywhere = pl.BlockSpec(memory_space=pl.ANY)
    vmem = pl.BlockSpec(memory_space=pltpu.VMEM)

    def array(*shape):
        return jax.ShapeDtypeStruct(shape, jnp.float32)

    def part(k):
        return array(parts[k + 1] - parts[k] + (skip if k == 0 else 0), columns)

    first_edge, last_edge = pl.pallas_call(
        prepare_kernel, out_shape=(array(q, LANES), array(q, LANES)), in_specs=[vmem], out_specs=(vmem, vmem)
    )(record)
    from_left = shifted(last_edge, "rcv", 1)
    from_right = shifted(first_edge, "rcv", -1)
    mine = jnp.concatenate([offsets, lengths]).astype(jnp.float32)
    wide = columns + 2 * LANES
    wide_first, wide_last, *own = pl.pallas_call(
        functools.partial(header_kernel, parts),
        out_shape=(array(ROWHALO, wide), array(ROWHALO + 8, wide)) + tuple(part(k) for k in range(4)),
        in_specs=[smem, smem, vmem, vmem, vmem],
        out_specs=(vmem,) * 6,
    )(offsets, lengths, record, from_left, from_right)
    to_odd = [(i, i + 1) for i in range(0, shots - 1, 2)]
    to_even = [(i + 1, i) for i in range(0, shots - 1, 2)]
    far = [shifted(x, "shot", -2) for x in own]
    passed = [lax.ppermute(x, "shot", to_odd) for x in far]
    given = [lax.ppermute(x, "shot", to_even) for x in own]
    second_last = shifted(mine, "shot", 2)
    top = shifted(wide_last, "shot", 1)
    bot = shifted(wide_first, "shot", -3)
    about = [second_last, top[ROWHALO, :2], mine, passed[0][HEAD, :2] + given[0][HEAD, :2], far[0][HEAD, :2]]
    params = jnp.stack(about).astype(jnp.int32)

    into, back = ring_matrices(columns)
    deep = window + 2 * PAD
    work = pltpu.VMEM((PLANES, deep, LANES), jnp.float32)

    def phase(out, arrays, waits, pieces, span):
        held = waits if out is None else [out] + waits
        return pl.pallas_call(
            functools.partial(deblend_kernel, (seg, columns, len(arrays)), pieces, span, len(held)),
            out_shape=array(1, window, columns),
            in_specs=[smem, smem, vmem, vmem] + [vmem] * len(arrays) + [anywhere] * len(held),
            out_specs=anywhere,
            input_output_aliases={} if out is None else {4 + len(arrays): 0},
            scratch_shapes=[
                pltpu.VMEM((PLANES, 3 * seg + 2 * PAD, LANES), jnp.float32),
                work, work, work, work,
                pltpu.VMEM((3, PLANES, STRIP + 32, LANES), jnp.float32),
                pltpu.VMEM((window, columns), jnp.float32),
                pltpu.SemaphoreType.DMA((window // BLOCK,)),
            ],
            compiler_params=pltpu.CompilerParams(vmem_limit_bytes=60 * 1024 * 1024),
        )(params, thresholds, into, back, *arrays, *held)

    def pieces_of(main, halo, segment, begin, end, start=0, parity=None):
        found = []
        while begin < end:
            quarter = begin // q
            until = min(end, (quarter + 1) * q)
            found.append((parity, main, halo, begin - start, until - begin, quarter, segment * seg + begin))
            begin = until
        return found

    def part_pieces(k, main, halo, segment, begin=None, end=None, parity=None):
        start = parts[k] - (skip if k == 0 else 0)
        begin = parts[k] if begin is None else begin
        return pieces_of(main, halo, segment, begin, parts[k + 1] if end is None else end, start, parity)

    blocks = window // BLOCK

    def mark(offset, rows):
        return jnp.clip((seg + rows - 28 - offset) // BLOCK, 0, blocks)

    def far_begin(offset):
        return jnp.minimum((2 * seg + 35 - offset) // 8 * 8 // BLOCK, blocks)

    def far_middle(offset):
        return jnp.clip((2 * seg + parts[2] - 28 - offset) // BLOCK, far_begin(offset), blocks)


    def takes_far(offset):
        return far_middle(offset) - far_begin(offset) >= 4

    def second(offset):
        near_count = mark(offset, 0)
        far_count = far_middle(offset) - far_begin(offset)
        is_far = takes_far(offset)
        return jnp.where(is_far, far_begin(offset), 0) * BLOCK, jnp.where(is_far, far_count, near_count)

    def third(offset):
        begin = jnp.where(takes_far(offset), 0, mark(offset, 0))
        return begin * BLOCK, mark(offset, parts[2]) - begin

    def fourth(offset):
        begin = jnp.where(takes_far(offset), far_middle(offset), far_begin(offset))
        return begin * BLOCK, blocks - begin

    def last(offset):
        begin = mark(offset, parts[2])
        last_row = jnp.minimum((2 * seg + 35 - offset) // 8 * 8, window)
        return begin * BLOCK, (last_row - begin * BLOCK + BLOCK - 1) // BLOCK

    def near_pieces(k, arrays, halo, begin=None):
        return part_pieces(k, arrays, halo, 1, begin, None, 1) + part_pieces(k, arrays + 1, halo + 1, 1, begin, None, 0)

    own_pieces = pieces_of(0, 1, 0, 0, seg)
    top_piece = (None, 2, None, 0, ROWHALO, QUARTERS - 1, -ROWHALO)
    out = phase(
        None, [record, own[0], top, far[0], far[1]], [],
        [top_piece] + own_pieces + part_pieces(0, 3, 3, 2) + part_pieces(1, 4, 3, 2), second,
    )
    out = phase(
        out, [record, own[0], top, passed[0], given[0], passed[1], given[1]], [],
        [top_piece] + own_pieces + near_pieces(0, 3, 3) + near_pieces(1, 5, 3), third,
    )
    out = phase(
        out, [far[0], far[1], far[2], far[3], bot], [],
        [piece for k in range(4) for piece in part_pieces(k, k, 0, 2)]
        + [(None, 4, None, 0, ROWHALO, 0, 3 * seg)], fourth,
    )
    return phase(
        out, [passed[0], given[0], passed[1], given[1], passed[2], given[2], passed[3], given[3], far[0], far[1]], [],
        near_pieces(1, 2, 0, parts[2] - 128) + near_pieces(2, 4, 0) + near_pieces(3, 6, 0)
        + part_pieces(0, 8, 8, 2) + part_pieces(1, 9, 8, 2, end=q),
        last,
    )


def solution(mesh):
    return jax.shard_map(
        on_device,
        mesh=mesh,
        in_specs=(P("shot", "rcv"), P("shot"), P("shot"), P()),
        out_specs=P("shot", None, "rcv"),
        check_vma=False,
    )
```

```python
import functools

import numpy as np
import jax
import jax.numpy as jnp
from jax import lax
from jax.experimental import pallas as pl
from jax.experimental.pallas import tpu as pltpu
from jax.sharding import PartitionSpec as P

LEVELS = 3
relax_step = 0.5

PLANES = 5
LANES = 128
RING = PLANES * LANES
EDGE = 32
QUARTERS = LANES // EDGE
HEAD = 128
PAD = 64
ROWHALO = 16
BLOCK = 64
STRIP = 64


def shifted(shard, axis, by):
    devices = lax.axis_size(axis)
    pairs = [(i, i + by) for i in range(devices) if 0 <= i + by < devices]
    return lax.ppermute(shard, axis, pairs)


def ring_matrices(columns):
    wide = columns + 2 * LANES
    into = np.zeros((wide, RING), np.float32)
    back = np.zeros((RING, columns), np.float32)

    def place(ring):
        return (ring % PLANES) * LANES + ring // PLANES

    for column in range(columns):
        into[column, place(column)] = relax_step
        back[place(column), column] = 1.0
    for quarter in range(LANES // EDGE):
        for i in range(EDGE):
            into[columns + quarter * EDGE + i, place(RING - EDGE + i)] = relax_step
            into[columns + LANES + quarter * EDGE + i, place(columns + i)] = relax_step
    return jnp.asarray(into, jnp.bfloat16), jnp.asarray(back, jnp.bfloat16)


def smooth_across(planes, dilation):
    rolled = {}

    def at(position):
        turns, plane = divmod(position, PLANES)
        if turns == 0:
            return planes[plane]
        if (turns, plane) not in rolled:
            rolled[turns, plane] = pltpu.roll(planes[plane], (-turns) % LANES, 1)
        return rolled[turns, plane]

    return [
        (at(k - 2 * dilation) + at(k + 2 * dilation))
        + 4.0 * (at(k - dilation) + at(k + dilation))
        + 6.0 * planes[k]
        for k in range(PLANES)
    ]


def limit(values, cut):
    return jnp.minimum(jnp.maximum(values, -cut), cut)


def pairs_of(first, count, body):
    def step(b, carry):
        body(pl.multiple_of(first + b * (2 * BLOCK), 8))
        return carry

    lax.fori_loop(0, (count + 1) // 2, step, 0)


def smooth_block(ref, start, rows, dilation, scale):
    centre, summed = [], []
    for k in range(PLANES):
        x = [ref[k, pl.ds(start + tap * dilation, rows), :] for tap in range(-2, 3)]
        centre.append(x[2])
        summed.append((x[0] + x[4]) + 4.0 * (x[1] + x[3]) + 6.0 * x[2])
    summed = smooth_across(summed, dilation)
    return centre, [s * w for s, w in zip(summed, scale)]


def deblend_kernel(geometry, pieces, halo_places, outer, span, operands, params, thr, *refs):
    seg, columns = geometry
    into_hbm, back_hbm, *sources = refs[:operands]
    out, into, back, ext, halos, beyond, gathered, c1, c2, f, strip, staged, sem, out_sem = refs[operands:]
    window = 2 * seg
    quarter_rows = seg // QUARTERS
    pair = 2 * BLOCK

    shots = lax.axis_size("shot")
    me = lax.axis_index("shot")
    rcv = lax.axis_index("rcv")
    offset = params[2, 0]
    live = params[2, 1]
    total = (shots - me) * seg - offset

    def shot(by):
        return by * seg + params[by + 2, 0] - offset, params[by + 2, 1]

    spans = [(pl.multiple_of(begin * BLOCK, 8), jnp.maximum(end - begin, 0)) for begin, end in span(offset)]
    some = sum(count for _, count in spans) > 0

    def reached(row, rows):
        found = False
        for low, count in spans:
            inside = (row < offset + low + count * BLOCK + 40) & (row + rows > offset + low - 40)
            found = found | ((count > 0) & inside)
        return found

    def copy_of(n, src, target):
        return pltpu.make_async_copy(src, target, sem.at[n])

    brought = [(0, None, into, some)]
    for main, first, rows, row in pieces:
        brought.append((main, (first, rows), ext.at[pl.ds(row, rows), :], reached(row, rows)))
    for segment, place in enumerate(halo_places):
        if place is not None:
            brought.append((place, (0, HEAD), halos.at[segment], some))
    if outer is not None:
        brought.append((outer[0], (0, ROWHALO), beyond, reached(outer[1], ROWHALO)))

    pl.when(some)(lambda: copy_of(0, into_hbm, into).start())
    for n, (place, part, target, wanted) in enumerate(brought):
        if part is not None:
            pl.when(wanted)(lambda: copy_of(n, sources[place].at[pl.ds(*part), :], target).start())
    pl.when(some)(lambda: copy_of(len(brought), back_hbm, back).start())

    lane = lax.broadcasted_iota(jnp.int32, (1, LANES), 1)
    has_right = jnp.where(rcv < lax.axis_size("rcv") - 1, 1.0, 0.0)
    has_left = jnp.where(rcv > 0, 1.0, 0.0)
    scale = []
    for k in range(PLANES):
        ring = lane * PLANES + k
        side = jnp.where(ring < columns + LANES // 2, has_right, has_left)
        scale.append(jnp.where(ring < columns, 1.0, side) * (1.0 / 256.0))
    strip[:, :, 0:16, :] = jnp.zeros((3, PLANES, 16, LANES), jnp.float32)
    strip[:, :, 16 + STRIP : 32 + STRIP, :] = jnp.zeros((3, PLANES, 16, LANES), jnp.float32)

    for n, (place, part, target, wanted) in enumerate(brought):
        pl.when(wanted)(lambda: copy_of(n, target, target).wait())

    def permute_in(main, left, right, quarter, row):
        mine = (lane // EDGE) == quarter
        lhs = [main] + [jnp.where(mine, x, 0.0) for x in (left, right)]
        lhs = jnp.concatenate([x.astype(jnp.bfloat16) for x in lhs], axis=1)
        result = jnp.dot(lhs, into[...], preferred_element_type=jnp.float32)
        for k in range(PLANES):
            gathered[0, k, pl.ds(PAD + row, main.shape[0]), :] = result[:, k * LANES : (k + 1) * LANES]

    def permute_quarter(i, carry):
        row = pl.multiple_of(i * quarter_rows, quarter_rows)
        segment = row // seg
        sides = []
        for side in range(2):
            lanes = [2 * side * LANES + at // HEAD * LANES for at in range(0, quarter_rows, HEAD)]
            sides.append(jnp.concatenate([halos[segment, :, at : at + LANES] for at in lanes], axis=0))
        permute_in(ext[pl.ds(row, quarter_rows), :], *sides, lax.rem(row, seg) // quarter_rows, row)
        return carry

    for low, count in spans:
        begin = jnp.clip((offset + low - 40) // quarter_rows, 0, 3 * QUARTERS)
        end = jnp.clip((offset + low + count * BLOCK + 40 + quarter_rows - 1) // quarter_rows, 0, 3 * QUARTERS)
        lax.fori_loop(begin, jnp.where(count > 0, end, begin), permute_quarter, 0)
    if outer is not None:

        @pl.when(reached(outer[1], ROWHALO))
        def _():
            quarter = QUARTERS - 1 if outer[1] < 0 else 0
            sides = [beyond[:, columns + side * LANES : columns + (side + 1) * LANES] for side in range(2)]
            permute_in(beyond[:, 0:columns], *sides, quarter, outer[1])

    def level_pass(source, shift, target, dilation, first, count):
        def body(at):
            _, summed = smooth_block(source, at + shift, pair, dilation, scale)
            for k in range(PLANES):
                target[k, pl.ds(at, pair), :] = summed[k]

        pairs_of(first, count, body)

    def shrunk(sweep, shift, at):
        centre, summed = smooth_block(c2, at, pair, 4, scale)
        for k in range(PLANES):
            x0 = gathered[sweep, k, pl.ds(at + shift, pair), :]
            x1 = c1[k, pl.ds(at, pair), :]
            x2 = centre[k]
            clipped = limit(x0 - x1, thr[0]) + limit(x1 - x2, thr[1]) + limit(x2 - summed[k], thr[2])
            yield k, x0, x0 - clipped

    def next_gathered(at):
        t = at - PAD + lax.broadcasted_iota(jnp.int32, (pair, LANES), 0)
        shots_live = jnp.zeros(t.shape, jnp.float32)
        for by in range(-2, 3):
            begin, length = shot(by)
            shots_live = shots_live + jnp.where((t >= begin) & (t < begin + length), 1.0, 0.0)
        own_live = jnp.where((t >= 0) & (t < live), 1.0, 0.0)
        inside = jnp.where(t < total, relax_step, 0.0)
        factor = own_live * (1.0 - inside * shots_live)
        for k, x0, value in shrunk(0, offset, at):
            f[k, pl.ds(at, pair), :] = value
            gathered[1, k, pl.ds(at, pair), :] = own_live * x0 + factor * value

    half = STRIP // 2

    def do_strip(by, at_end):
        begin, length = shot(by)
        p = begin + jnp.where(at_end, length, 0)
        t = p - half + lax.broadcasted_iota(jnp.int32, (STRIP, LANES), 0)
        in_live = jnp.where((t >= begin) & (t < begin + length), 1.0, 0.0)
        in_window = jnp.where((t >= begin) & (t < begin + window), 1.0, 0.0)
        for k in range(PLANES):
            strip[0, k, 16 : 16 + STRIP, :] = gathered[0, k, pl.ds(PAD + offset + p - half, STRIP), :] * in_live
        for j in range(2):
            _, summed = smooth_block(strip.at[j], 16, STRIP, 2**j, scale)
            for k in range(PLANES):
                strip[j + 1, k, 16 : 16 + STRIP, :] = summed[k] * in_window
        mid = half
        _, summed = smooth_block(strip.at[2], mid, 32, 4, scale)
        t = p - 16 + lax.broadcasted_iota(jnp.int32, (32, LANES), 0)
        in_window = jnp.where((t >= begin) & (t < begin + window), 1.0, 0.0)
        near_edge = (t >= begin) & (t < begin + length) & (t >= p - 14) & (t < p + 14)
        own_live = (t >= 0) & (t < live)
        inside = jnp.where(t < total, -relax_step, 0.0)
        weight = jnp.where(near_edge & own_live, inside + jnp.where(by == 0, 1.0, 0.0), 0.0)
        for k in range(PLANES):
            x0 = strip[0, k, mid : mid + 32, :]
            x1 = strip[1, k, mid : mid + 32, :]
            x2 = strip[2, k, mid : mid + 32, :]
            x3 = summed[k] * in_window
            clipped = limit(x0 - x1, thr[0]) + limit(x1 - x2, thr[1]) + limit(x2 - x3, thr[2])
            where = pl.ds(PAD + p - 16, 32)
            gathered[1, k, where, :] = gathered[1, k, where, :] + weight * (x0 - clipped - f[k, where, :])

    def out_copy(low, i):
        rows = pl.ds(pl.multiple_of(low + i * BLOCK, 8), BLOCK)
        return pltpu.make_async_copy(staged.at[rows, :], out.at[0, rows, :], out_sem.at[i])

    def estimate(low, count, at):
        t = at - PAD + lax.broadcasted_iota(jnp.int32, (pair, LANES), 0)
        own_live = jnp.where(t < live, 1.0, 0.0)
        high, rest = [], []
        for k, _, value in shrunk(1, 0, at):
            x = own_live * value
            h = x.astype(jnp.bfloat16)
            high.append(h)
            rest.append((x - h.astype(jnp.float32)).astype(jnp.bfloat16))
        both = jnp.concatenate([jnp.concatenate(high, axis=1), jnp.concatenate(rest, axis=1)], axis=0)
        result = jnp.dot(both, back[...], preferred_element_type=jnp.float32)
        staged[pl.ds(pl.multiple_of(at - PAD, 8), pair), :] = result[:pair] + result[pair:]
        i = (at - PAD - low) // BLOCK
        out_copy(low, i).start()
        pl.when(i + 1 < count)(lambda: out_copy(low, i + 1).start())

    def clear_edges(ref):
        ref[:, PAD - 16 : PAD, :] = jnp.zeros((PLANES, 16, LANES), jnp.float32)
        ref[:, PAD + window : PAD + window + 16, :] = jnp.zeros((PLANES, 16, LANES), jnp.float32)

    def process(low, count):
        high = low + count * BLOCK
        first = PAD + low
        wider, many = first - BLOCK // 2, count + 1

        def strip_step(i, carry):
            by, at_end = i // 2 - 2, i % 2 == 1
            begin, length = shot(by)
            p = begin + jnp.where(at_end, length, 0)
            begins_at = jnp.where(at_end, p - 14, p)
            bottom = jnp.maximum(low - 14, 0)
            top = jnp.minimum(high + 14, live)

            @pl.when((length > 0) & (begins_at + 14 > bottom) & (begins_at < top))
            def _():
                do_strip(by, at_end)

            return carry

        level_pass(gathered.at[0], offset, c1, 1, wider, many)
        level_pass(c1, 0, c2, 2, wider, many)
        pairs_of(wider, many, next_gathered)
        lax.fori_loop(1, 10, strip_step, 0)
        clear_edges(gathered.at[1])
        level_pass(gathered.at[1], 0, c1, 1, wider, many)
        clear_edges(c1)
        level_pass(c1, 0, c2, 2, wider, many)
        clear_edges(c2)
        pairs_of(first, count, lambda at: estimate(low, count, at))

        def wait(i, carry):
            out_copy(low, i).wait()
            return carry

        lax.fori_loop(0, count, wait, 0)

    pl.when(some)(lambda: copy_of(len(brought), back, back).wait())

    def span_step(i, carry):
        low, count = spans[0]
        if len(spans) > 1:
            low, count = jnp.where(i == 0, low, spans[1][0]), jnp.where(i == 0, count, spans[1][1])
        pl.when(count > 0)(lambda: process(pl.multiple_of(low, 8), count))
        return carry

    lax.fori_loop(0, len(spans), span_step, 0)


def prepare_kernel(record, first_edge, last_edge):
    seg, columns = record.shape
    quarter = seg // QUARTERS
    lane = lax.broadcasted_iota(jnp.int32, (1, LANES), 1)
    for out, start, inner in ((first_edge, 0, 0), (last_edge, columns - LANES, LANES - EDGE)):
        packed = jnp.zeros((quarter, LANES), jnp.float32)
        for q in range(QUARTERS):
            rows = record[q * quarter : (q + 1) * quarter, start : start + LANES].astype(jnp.float32)
            turn = (q * EDGE - inner) % LANES
            packed = jnp.where(lane // EDGE == q, pltpu.roll(rows, turn, 1) if turn else rows, packed)
        out[...] = packed


def header_kernel(parts, offsets, lengths, record, left, right, wide_first, wide_last, *own):
    seg, columns = record.shape
    quarter = seg // QUARTERS
    lane = lax.broadcasted_iota(jnp.int32, (8, LANES), 1)
    about = jnp.where(lane == 0, offsets[0], jnp.where(lane == 1, lengths[0], 0)).astype(jnp.float32)
    first = own[0]
    for side, halo in enumerate((left, right)):
        for part in range(quarter // HEAD):
            at = (2 * side + part) * LANES
            first[0:HEAD, at : at + LANES] = halo[part * HEAD : (part + 1) * HEAD, :]
    first[HEAD : HEAD + 8, :] = jnp.concatenate([about] * (columns // LANES), axis=1)
    first[HEAD + 8 :, :] = record[0 : parts[1], :].astype(jnp.float32)
    for k in range(1, len(own)):
        own[k][...] = record[parts[k] : parts[k + 1], :].astype(jnp.float32)
    wide_first[:, 0:columns] = record[0:ROWHALO, :].astype(jnp.float32)
    wide_last[0:ROWHALO, 0:columns] = record[seg - ROWHALO : seg, :].astype(jnp.float32)
    for side, halo in enumerate((left, right)):
        at = columns + side * LANES
        wide_first[:, at : at + LANES] = halo[0:ROWHALO, :]
        wide_last[0:ROWHALO, at : at + LANES] = halo[quarter - ROWHALO : quarter, :]
    wide_last[ROWHALO:, :] = jnp.concatenate([about] * (columns // LANES + 2), axis=1)


def pass_on_kernel(unread, own, far, *refs):
    sent, sem = refs[unread], refs[-1]
    odd = lax.rem(lax.axis_index("shot"), 2) == 1
    pl.when(odd)(lambda: pltpu.make_async_copy(own, sent, sem).start())
    pl.when(jnp.logical_not(odd))(lambda: pltpu.make_async_copy(far, sent, sem).start())
    pltpu.make_async_copy(own, sent, sem).wait()


def shots_kernel(second_last, last, mine, following, second, out):
    lane = lax.broadcasted_iota(jnp.int32, (8, LANES), 1)
    row = lax.broadcasted_iota(jnp.int32, (8, LANES), 0)
    found = jnp.zeros((8, LANES), jnp.float32)
    for n, pair in enumerate((second_last, last, mine, following, second)):
        if n in (0, 2):
            value = jnp.where(lane == 0, pair[0], pair[1])
        else:
            value = pair[0:1, :]
        found = jnp.where(row == n, value, found)
    out[...] = found.astype(jnp.int32)


def on_device(record, offsets, lengths, thresholds):
    seg, columns = record.shape
    window = 2 * seg
    shots = lax.axis_size("shot")
    q = seg // QUARTERS
    skip = HEAD + 8
    step = (seg + skip + 4 * 16 - 1) // (4 * 16) * 16
    parts = [0] + [seg - k * step for k in (3, 2, 1, 0)]
    swap = [(i, i ^ 1) for i in range(shots) if i ^ 1 < shots]
    smem = pl.BlockSpec(memory_space=pltpu.SMEM)
    anywhere = pl.BlockSpec(memory_space=pl.ANY)
    vmem = pl.BlockSpec(memory_space=pltpu.VMEM)

    def array(*shape):
        return jax.ShapeDtypeStruct(shape, jnp.float32)

    def part(k):
        return array(parts[k + 1] - parts[k] + (skip if k == 0 else 0), columns)

    first_edge, last_edge = pl.pallas_call(
        prepare_kernel, out_shape=(array(q, LANES), array(q, LANES)), in_specs=[vmem], out_specs=(vmem, vmem)
    )(record)
    from_left = shifted(last_edge, "rcv", 1)
    from_right = shifted(first_edge, "rcv", -1)
    mine = jnp.concatenate([offsets, lengths]).astype(jnp.float32)
    wide = columns + 2 * LANES
    def after(x, *others):
        return pl.pallas_call(
            lambda *refs: None,
            out_shape=jax.ShapeDtypeStruct(x.shape, x.dtype),
            in_specs=[anywhere] * (1 + len(others)),
            out_specs=anywhere,
            input_output_aliases={0: 0},
        )(x, *others)

    wide_first, wide_last, *own = pl.pallas_call(
        functools.partial(header_kernel, parts),
        out_shape=(array(ROWHALO, wide), array(ROWHALO + 8, wide)) + tuple(part(k) for k in range(4)),
        in_specs=[smem, smem, vmem, vmem, vmem],
        out_specs=(vmem,) * 6,
    )(offsets, lengths, record, from_left, from_right)
    swap = [(i, i ^ 1) for i in range(shots) if i ^ 1 < shots]
    far, near = [None] * 4, [None] * 4
    second_last = shifted(mine, "shot", 2)
    top = shifted(wide_last, "shot", 1)
    bot = shifted(wide_first, "shot", -3)
    far[0] = shifted(own[0], "shot", -2)
    own[1] = after(own[1], top)
    far[1] = shifted(own[1], "shot", -2)

    def pass_on(k, *others):
        ahead = [own[k + 2]] if k + 2 < 4 else []
        sent, *ahead = pl.pallas_call(
            functools.partial(pass_on_kernel, len(ahead) + len(others)),
            out_shape=(part(k),) + tuple(array(*x.shape) for x in ahead),
            in_specs=[anywhere] * (2 + len(ahead) + len(others)),
            out_specs=(vmem,) + (anywhere,) * len(ahead),
            input_output_aliases={2: 1} if ahead else {},
            scratch_shapes=[pltpu.SemaphoreType.DMA],
        )(own[k], far[k], *ahead, *others)
        near[k] = lax.ppermute(sent, "shot", swap)
        if ahead:
            own[k + 2] = ahead[0]
            far[k + 2] = shifted(own[k + 2], "shot", -2)

    pass_on(0)
    pass_on(1, near[0], second_last, bot)

    def corner(row):
        return pl.BlockSpec((8, LANES), lambda _: (row // 8, 0))

    params = pl.pallas_call(
        shots_kernel,
        grid=(1,),
        out_shape=jax.ShapeDtypeStruct((8, LANES), jnp.int32),
        in_specs=[smem, corner(ROWHALO), smem, corner(HEAD), corner(HEAD)],
        out_specs=vmem,
    )(second_last, top, mine, near[0], far[0])

    into, back = ring_matrices(columns)
    work = pltpu.VMEM((PLANES, window + 4 * PAD, LANES), jnp.float32)

    def phase(out, arrays, pieces, halo_places, outer, span):
        held = [] if out is None else [out]
        return pl.pallas_call(
            functools.partial(
                deblend_kernel, (seg, columns), pieces, halo_places, outer, span, 2 + len(arrays) + len(held)
            ),
            out_shape=array(1, window, columns),
            in_specs=[smem, smem] + [anywhere] * (2 + len(arrays) + len(held)),
            out_specs=anywhere,
            input_output_aliases={} if out is None else {4 + len(arrays): 0},
            scratch_shapes=[
                pltpu.VMEM(into.shape, into.dtype),
                pltpu.VMEM(back.shape, back.dtype),
                pltpu.VMEM((3 * seg, columns), jnp.float32),
                pltpu.VMEM((3, HEAD, columns), jnp.float32),
                pltpu.VMEM((ROWHALO, wide), jnp.float32),
                pltpu.VMEM((2, PLANES, 3 * seg + 4 * PAD, LANES), jnp.float32),
                work, work, work,
                pltpu.VMEM((3, PLANES, STRIP + 32, LANES), jnp.float32),
                pltpu.VMEM((window + BLOCK, columns), jnp.float32),
                pltpu.SemaphoreType.DMA((len(pieces) + 6,)),
                pltpu.SemaphoreType.DMA((window // BLOCK,)),
            ],
            compiler_params=pltpu.CompilerParams(vmem_limit_bytes=60 * 1024 * 1024),
        )(params, thresholds, into, back, *arrays, *held)

    def part_piece(k, main, segment):
        return (main, skip if k == 0 else 0, parts[k + 1] - parts[k], segment * seg + parts[k])

    blocks = window // BLOCK
    cap = 9

    def mark(offset, rows):
        return jnp.clip((seg + rows - 28 - offset) // BLOCK, 0, blocks)

    def far_begin(offset):
        return jnp.minimum((2 * seg + 35 - offset) // 8 * 8 // BLOCK, blocks)

    def far_middle(offset):
        return jnp.clip((2 * seg + parts[2] - 28 - offset) // BLOCK, far_begin(offset), blocks)

    def takes_far(offset):
        return far_middle(offset) - far_begin(offset) >= 4

    def first(offset):
        is_far = takes_far(offset)
        begin = jnp.where(is_far, far_begin(offset), 0)
        return [(begin, jnp.where(is_far, far_middle(offset), jnp.minimum(mark(offset, 0), cap)))]

    def second(offset):
        begin = jnp.where(takes_far(offset), 0, first(offset)[0][1])
        return [(begin, jnp.minimum(mark(offset, parts[2]), begin + cap))]

    def third(offset):
        is_far = takes_far(offset)
        return [(jnp.where(is_far, far_middle(offset), far_begin(offset)), blocks)]

    def last(offset):
        bridged = (jnp.minimum((2 * seg + 35 - offset) // 8 * 8, window) + BLOCK - 1) // BLOCK
        return [(second(offset)[0][1], bridged)]

    def every(places, segment):
        return [part_piece(k, place, segment) for k, place in enumerate(places)]

    own_pieces = every(range(4), 0)
    out = phase(None, [*own, top, far[0], far[1]], own_pieces + every((5, 6), 2), (0, None, 5), (4, -ROWHALO), first)
    pass_on(2, out, near[1])
    out = phase(
        out, [*own, top, near[0], near[1]], own_pieces + every((5, 6), 1), (0, 5, None), (4, -ROWHALO), second
    )
    pass_on(3, out, near[2])
    out = phase(out, [*far, bot], every(range(4), 2), (None, None, 0), (4, 3 * seg), third)
    return phase(
        out, [own[0], own[3], *near, far[0], far[1]],
        [part_piece(3, 1, 0)] + every(range(2, 6), 1) + every((6, 7), 2), (0, 2, 6), None, last,
    )


def solution(mesh):
    return jax.shard_map(
        on_device,
        mesh=mesh,
        in_specs=(P("shot", "rcv"), P("shot"), P("shot"), P()),
        out_specs=P("shot", None, "rcv"),
        check_vma=False,
    )
```

```python
import functools

import numpy as np
import jax
import jax.numpy as jnp
from jax import lax
from jax.experimental import pallas as pl
from jax.experimental.pallas import tpu as pltpu
from jax.sharding import PartitionSpec as P

LEVELS = 3
relax_step = 0.5

PLANES = 5
LANES = 128
RING = PLANES * LANES
HALF = LANES // 2
EDGE = 32
QUARTERS = LANES // EDGE
HEAD = 128
PAD = 64
ROWHALO = 16
BLOCK = 64
STRIP = 64


def shifted(shard, axis, by):
    devices = lax.axis_size(axis)
    pairs = [(i, i + by) for i in range(devices) if 0 <= i + by < devices]
    return lax.ppermute(shard, axis, pairs)


def ring_matrices(columns):
    wide = columns + 2 * LANES
    into = np.zeros((wide, RING), np.float32)
    back = np.zeros((RING, columns), np.float32)

    def place(ring):
        pair, side = divmod(ring, 2)
        return (pair % PLANES) * LANES + side * HALF + pair // PLANES

    for column in range(columns):
        into[column, place(EDGE + column)] = relax_step
        back[place(EDGE + column), column] = 1.0
    for quarter in range(LANES // EDGE):
        for i in range(EDGE):
            into[columns + quarter * EDGE + i, place(i)] = relax_step
            into[columns + LANES + quarter * EDGE + i, place(EDGE + columns + i)] = relax_step
    return jnp.asarray(into, jnp.bfloat16), jnp.asarray(back, jnp.bfloat16)


def smooth_across(planes, dilation):
    if dilation == 1:
        lane = lax.broadcasted_iota(jnp.int32, planes[0].shape, 1)
        other = [pltpu.roll(x, HALF, 1) for x in planes]
        before = [pltpu.roll(planes[-1], HALF + 1, 1)] + other[:-1]
        after = other[1:] + [pltpu.roll(planes[0], HALF - 1, 1)]
        two_before = [pltpu.roll(planes[-1], 1, 1)] + planes[:-1]
        two_after = planes[1:] + [pltpu.roll(planes[0], LANES - 1, 1)]
        return [
            (two_before[k] + two_after[k])
            + 4.0 * (other[k] + jnp.where(lane < HALF, before[k], after[k]))
            + 6.0 * planes[k]
            for k in range(PLANES)
        ]
    rolled = {}
    pairs = dilation // 2

    def at(position):
        turns, plane = divmod(position, PLANES)
        if turns == 0:
            return planes[plane]
        if (turns, plane) not in rolled:
            rolled[turns, plane] = pltpu.roll(planes[plane], (-turns) % LANES, 1)
        return rolled[turns, plane]

    return [
        (at(k - 2 * pairs) + at(k + 2 * pairs)) + 4.0 * (at(k - pairs) + at(k + pairs)) + 6.0 * planes[k]
        for k in range(PLANES)
    ]


def limit(values, cut):
    return jnp.minimum(jnp.maximum(values, -cut), cut)


def pairs_of(first, count, body):
    def step(b, carry):
        body(pl.multiple_of(first + b * (2 * BLOCK), 8))
        return carry

    lax.fori_loop(0, (count + 1) // 2, step, 0)


def smooth_block(ref, start, rows, dilation, scale):
    centre, summed = [], []
    for k in range(PLANES):
        x = [ref[k, pl.ds(start + tap * dilation, rows), :] for tap in range(-2, 3)]
        centre.append(x[2])
        summed.append((x[0] + x[4]) + 4.0 * (x[1] + x[3]) + 6.0 * x[2])
    summed = smooth_across(summed, dilation)
    return centre, [s * w for s, w in zip(summed, scale)]


def deblend_kernel(geometry, pieces, halo_places, outers, span, operands, params, thr, *refs):
    seg, columns = geometry
    into_hbm, back_hbm, *sources = refs[:operands]
    out, into, back, ext, halos, beyond, gathered, c1, c2, f, strip, staged, sem, out_sem = refs[operands:]
    window = 2 * seg
    quarter_rows = seg // QUARTERS
    pair = 2 * BLOCK

    shots = lax.axis_size("shot")
    me = lax.axis_index("shot")
    rcv = lax.axis_index("rcv")
    offset = params[2, 0]
    live = params[2, 1]
    total = (shots - me) * seg - offset

    def shot(by):
        return by * seg + params[by + 2, 0] - offset, params[by + 2, 1]

    spans = [(pl.multiple_of(begin * BLOCK, 8), jnp.maximum(end - begin, 0)) for begin, end in span(offset)]
    some = sum(count for _, count in spans) > 0

    def reached(row, rows):
        found = False
        for low, count in spans:
            inside = (row < offset + low + count * BLOCK + 40) & (row + rows > offset + low - 40)
            found = found | ((count > 0) & inside)
        return found

    def copy_of(n, src, target):
        return pltpu.make_async_copy(src, target, sem.at[n])

    brought = [(0, None, into, some)]
    for main, first, rows, row in pieces:
        brought.append((main, (first, rows), ext.at[pl.ds(row, rows), :], reached(row, rows)))
    for segment, place in enumerate(halo_places):
        if place is not None:
            brought.append((place, (0, HEAD), halos.at[segment], some))
    for n, (place, row) in enumerate(outers):
        brought.append((place, (0, ROWHALO), beyond.at[n], reached(row, ROWHALO)))

    pl.when(some)(lambda: copy_of(0, into_hbm, into).start())
    for n, (place, part, target, wanted) in enumerate(brought):
        if part is not None:
            pl.when(wanted)(lambda: copy_of(n, sources[place].at[pl.ds(*part), :], target).start())
    pl.when(some)(lambda: copy_of(len(brought), back_hbm, back).start())

    lane = lax.broadcasted_iota(jnp.int32, (1, LANES), 1)
    has_right = jnp.where(rcv < lax.axis_size("rcv") - 1, 1.0, 0.0)
    has_left = jnp.where(rcv > 0, 1.0, 0.0)
    scale = []
    for k in range(PLANES):
        ring = 2 * (lane % HALF * PLANES + k) + lane // HALF
        side = jnp.where(ring < EDGE, has_left, has_right)
        scale.append(jnp.where((ring >= EDGE) & (ring < EDGE + columns), 1.0, side) * (1.0 / 256.0))
    strip[:, :, 0:16, :] = jnp.zeros((3, PLANES, 16, LANES), jnp.float32)
    strip[:, :, 16 + STRIP : 32 + STRIP, :] = jnp.zeros((3, PLANES, 16, LANES), jnp.float32)

    for n, (place, part, target, wanted) in enumerate(brought):
        pl.when(wanted)(lambda: copy_of(n, target, target).wait())

    def permute_in(main, left, right, quarter, row):
        mine = (lane // EDGE) == quarter
        lhs = [main] + [jnp.where(mine, x, 0.0) for x in (left, right)]
        lhs = jnp.concatenate([x.astype(jnp.bfloat16) for x in lhs], axis=1)
        result = jnp.dot(lhs, into[...], preferred_element_type=jnp.float32)
        for k in range(PLANES):
            gathered[0, k, pl.ds(PAD + row, main.shape[0]), :] = result[:, k * LANES : (k + 1) * LANES]

    def permute_quarter(i, carry):
        row = pl.multiple_of(i * quarter_rows, quarter_rows)
        segment = row // seg
        sides = []
        for side in range(2):
            lanes = [2 * side * LANES + at // HEAD * LANES for at in range(0, quarter_rows, HEAD)]
            sides.append(jnp.concatenate([halos[segment, :, at : at + LANES] for at in lanes], axis=0))
        permute_in(ext[pl.ds(row, quarter_rows), :], *sides, lax.rem(row, seg) // quarter_rows, row)
        return carry

    for low, count in spans:
        begin = jnp.clip((offset + low - 40) // quarter_rows, 0, 3 * QUARTERS)
        end = jnp.clip((offset + low + count * BLOCK + 40 + quarter_rows - 1) // quarter_rows, 0, 3 * QUARTERS)
        lax.fori_loop(begin, jnp.where(count > 0, end, begin), permute_quarter, 0)
    for n, (place, row) in enumerate(outers):

        @pl.when(reached(row, ROWHALO))
        def _():
            sides = [beyond[n, :, columns + side * LANES : columns + (side + 1) * LANES] for side in range(2)]
            permute_in(beyond[n, :, 0:columns], *sides, QUARTERS - 1 if row < 0 else 0, row)

    def level_pass(source, shift, target, dilation, first, count):
        def body(at):
            _, summed = smooth_block(source, at + shift, pair, dilation, scale)
            for k in range(PLANES):
                target[k, pl.ds(at, pair), :] = summed[k]

        pairs_of(first, count, body)

    def shrunk(sweep, shift, at):
        centre, summed = smooth_block(c2, at, pair, 4, scale)
        for k in range(PLANES):
            x0 = gathered[sweep, k, pl.ds(at + shift, pair), :]
            x1 = c1[k, pl.ds(at, pair), :]
            x2 = centre[k]
            clipped = limit(x0 - x1, thr[0]) + limit(x1 - x2, thr[1]) + limit(x2 - summed[k], thr[2])
            yield k, x0, x0 - clipped

    def next_gathered(at):
        t = at - PAD + lax.broadcasted_iota(jnp.int32, (pair, LANES), 0)
        shots_live = jnp.zeros(t.shape, jnp.float32)
        for by in range(-2, 3):
            begin, length = shot(by)
            shots_live = shots_live + jnp.where((t >= begin) & (t < begin + length), 1.0, 0.0)
        own_live = jnp.where((t >= 0) & (t < live), 1.0, 0.0)
        inside = jnp.where(t < total, relax_step, 0.0)
        factor = own_live * (1.0 - inside * shots_live)
        for k, x0, value in shrunk(0, offset, at):
            f[k, pl.ds(at, pair), :] = value
            gathered[1, k, pl.ds(at, pair), :] = own_live * x0 + factor * value

    half = STRIP // 2

    def do_strip(by, at_end):
        begin, length = shot(by)
        p = begin + jnp.where(at_end, length, 0)
        t = p - half + lax.broadcasted_iota(jnp.int32, (STRIP, LANES), 0)
        in_live = jnp.where((t >= begin) & (t < begin + length), 1.0, 0.0)
        in_window = jnp.where((t >= begin) & (t < begin + window), 1.0, 0.0)
        for k in range(PLANES):
            strip[0, k, 16 : 16 + STRIP, :] = gathered[0, k, pl.ds(PAD + offset + p - half, STRIP), :] * in_live
        for j in range(2):
            _, summed = smooth_block(strip.at[j], 16, STRIP, 2**j, scale)
            for k in range(PLANES):
                strip[j + 1, k, 16 : 16 + STRIP, :] = summed[k] * in_window
        mid = half
        _, summed = smooth_block(strip.at[2], mid, 32, 4, scale)
        t = p - 16 + lax.broadcasted_iota(jnp.int32, (32, LANES), 0)
        in_window = jnp.where((t >= begin) & (t < begin + window), 1.0, 0.0)
        near_edge = (t >= begin) & (t < begin + length) & (t >= p - 14) & (t < p + 14)
        own_live = (t >= 0) & (t < live)
        inside = jnp.where(t < total, -relax_step, 0.0)
        weight = jnp.where(near_edge & own_live, inside + jnp.where(by == 0, 1.0, 0.0), 0.0)
        for k in range(PLANES):
            x0 = strip[0, k, mid : mid + 32, :]
            x1 = strip[1, k, mid : mid + 32, :]
            x2 = strip[2, k, mid : mid + 32, :]
            x3 = summed[k] * in_window
            clipped = limit(x0 - x1, thr[0]) + limit(x1 - x2, thr[1]) + limit(x2 - x3, thr[2])
            where = pl.ds(PAD + p - 16, 32)
            gathered[1, k, where, :] = gathered[1, k, where, :] + weight * (x0 - clipped - f[k, where, :])

    def out_copy(low, i):
        rows = pl.ds(pl.multiple_of(low + i * BLOCK, 8), BLOCK)
        return pltpu.make_async_copy(staged.at[rows, :], out.at[0, rows, :], out_sem.at[i])

    def estimate(low, count, at):
        t = at - PAD + lax.broadcasted_iota(jnp.int32, (pair, LANES), 0)
        own_live = jnp.where(t < live, 1.0, 0.0)
        high, rest = [], []
        for k, _, value in shrunk(1, 0, at):
            x = own_live * value
            h = x.astype(jnp.bfloat16)
            high.append(h)
            rest.append((x - h.astype(jnp.float32)).astype(jnp.bfloat16))
        both = jnp.concatenate([jnp.concatenate(high, axis=1), jnp.concatenate(rest, axis=1)], axis=0)
        result = jnp.dot(both, back[...], preferred_element_type=jnp.float32)
        staged[pl.ds(pl.multiple_of(at - PAD, 8), pair), :] = result[:pair] + result[pair:]
        i = (at - PAD - low) // BLOCK
        out_copy(low, i).start()
        pl.when(i + 1 < count)(lambda: out_copy(low, i + 1).start())

    def clear_edges(ref):
        ref[:, PAD - 16 : PAD, :] = jnp.zeros((PLANES, 16, LANES), jnp.float32)
        ref[:, PAD + window : PAD + window + 16, :] = jnp.zeros((PLANES, 16, LANES), jnp.float32)

    def process(low, count):
        high = low + count * BLOCK
        first = PAD + low
        wider, many = first - BLOCK // 2, count + 1

        def strip_step(i, carry):
            by, at_end = i // 2 - 2, i % 2 == 1
            begin, length = shot(by)
            p = begin + jnp.where(at_end, length, 0)
            begins_at = jnp.where(at_end, p - 14, p)
            bottom = jnp.maximum(low - 14, 0)
            top = jnp.minimum(high + 14, live)

            @pl.when((length > 0) & (begins_at + 14 > bottom) & (begins_at < top))
            def _():
                do_strip(by, at_end)

            return carry

        level_pass(gathered.at[0], offset, c1, 1, wider, many)
        level_pass(c1, 0, c2, 2, wider, many)
        pairs_of(wider, many, next_gathered)
        lax.fori_loop(1, 10, strip_step, 0)
        clear_edges(gathered.at[1])
        level_pass(gathered.at[1], 0, c1, 1, wider, many)
        clear_edges(c1)
        level_pass(c1, 0, c2, 2, wider, many)
        clear_edges(c2)
        pairs_of(first, count, lambda at: estimate(low, count, at))

        def wait(i, carry):
            out_copy(low, i).wait()
            return carry

        lax.fori_loop(0, count, wait, 0)

    pl.when(some)(lambda: copy_of(len(brought), back, back).wait())

    def span_step(i, carry):
        low, count = spans[0]
        if len(spans) > 1:
            low, count = jnp.where(i == 0, low, spans[1][0]), jnp.where(i == 0, count, spans[1][1])
        pl.when(count > 0)(lambda: process(pl.multiple_of(low, 8), count))
        return carry

    lax.fori_loop(0, len(spans), span_step, 0)


def prepare_kernel(first_columns, last_columns, first_edge, last_edge):
    quarter = first_edge.shape[0]
    lane = lax.broadcasted_iota(jnp.int32, (1, LANES), 1)
    for out, source, inner in ((first_edge, first_columns, 0), (last_edge, last_columns, LANES - EDGE)):
        packed = jnp.zeros((quarter, LANES), jnp.float32)
        for q in range(QUARTERS):
            rows = source[q * quarter : (q + 1) * quarter, :].astype(jnp.float32)
            turn = (q * EDGE - inner) % LANES
            packed = jnp.where(lane // EDGE == q, pltpu.roll(rows, turn, 1) if turn else rows, packed)
        out[...] = packed


def header_kernel(offsets, lengths, first_rows, last_rows, left, right, own, wide_first, wide_last):
    quarter = left.shape[0]
    columns = own.shape[1]
    lane = lax.broadcasted_iota(jnp.int32, (8, LANES), 1)
    about = jnp.where(lane == 0, offsets[0], jnp.where(lane == 1, lengths[0], 0)).astype(jnp.float32)
    for side, halo in enumerate((left, right)):
        for part in range(quarter // HEAD):
            at = (2 * side + part) * LANES
            own[0:HEAD, at : at + LANES] = halo[part * HEAD : (part + 1) * HEAD, :]
    own[HEAD : HEAD + 8, :] = jnp.concatenate([about] * (columns // LANES), axis=1)
    own[HEAD + 8 :, :] = first_rows[...].astype(jnp.float32)
    wide_first[:, 0:columns] = first_rows[0:ROWHALO, :].astype(jnp.float32)
    wide_last[0:ROWHALO, 0:columns] = last_rows[...].astype(jnp.float32)
    for side, halo in enumerate((left, right)):
        at = columns + side * LANES
        wide_first[:, at : at + LANES] = halo[0:ROWHALO, :]
        wide_last[0:ROWHALO, at : at + LANES] = halo[quarter - ROWHALO : quarter, :]
    wide_last[ROWHALO:, :] = jnp.concatenate([about] * (columns // LANES + 2), axis=1)


def widen_kernel(begins, record, wait, *own):
    for begin, out in zip(begins, own):
        out[...] = record[begin : begin + out.shape[0], :].astype(jnp.float32)


def pass_on_kernel(unread, own, far, *refs):
    sent, sem = refs[unread], refs[-1]
    odd = lax.rem(lax.axis_index("shot"), 2) == 1
    pl.when(odd)(lambda: pltpu.make_async_copy(own, sent, sem).start())
    pl.when(jnp.logical_not(odd))(lambda: pltpu.make_async_copy(far, sent, sem).start())
    pltpu.make_async_copy(own, sent, sem).wait()


def shots_kernel(second_last, last, mine, following, second, out):
    lane = lax.broadcasted_iota(jnp.int32, (8, LANES), 1)
    row = lax.broadcasted_iota(jnp.int32, (8, LANES), 0)
    found = jnp.zeros((8, LANES), jnp.float32)
    for n, pair in enumerate((second_last, last, mine, following, second)):
        if n in (0, 2):
            value = jnp.where(lane == 0, pair[0], pair[1])
        else:
            value = pair[0:1, :]
        found = jnp.where(row == n, value, found)
    out[...] = found.astype(jnp.int32)


def on_device(record, offsets, lengths, thresholds):
    seg, columns = record.shape
    window = 2 * seg
    shots = lax.axis_size("shot")
    q = seg // QUARTERS
    skip = HEAD + 8
    step = (seg + skip + 4 * 16 - 1) // (4 * 16) * 16
    parts = [0] + [seg - k * step for k in (3, 2, 1, 0)]
    swap = [(i, i ^ 1) for i in range(shots) if i ^ 1 < shots]
    smem = pl.BlockSpec(memory_space=pltpu.SMEM)
    anywhere = pl.BlockSpec(memory_space=pl.ANY)
    vmem = pl.BlockSpec(memory_space=pltpu.VMEM)

    def array(*shape):
        return jax.ShapeDtypeStruct(shape, jnp.float32)

    def part(k):
        return array(parts[k + 1] - parts[k] + (skip if k == 0 else 0), columns)

    def window_of(rows, width, row, column):
        return pl.BlockSpec((rows, width), lambda _: (row, column))

    first_edge, last_edge = pl.pallas_call(
        prepare_kernel,
        grid=(1,),
        out_shape=(array(q, LANES), array(q, LANES)),
        in_specs=[window_of(seg, LANES, 0, 0), window_of(seg, LANES, 0, columns // LANES - 1)],
        out_specs=(vmem, vmem),
    )(record, record)
    from_left = shifted(last_edge, "rcv", 1)
    from_right = shifted(first_edge, "rcv", -1)
    mine = jnp.concatenate([offsets, lengths]).astype(jnp.float32)
    wide = columns + 2 * LANES
    first_part, wide_first, wide_last = pl.pallas_call(
        header_kernel,
        grid=(1,),
        out_shape=(part(0), array(ROWHALO, wide), array(ROWHALO + 8, wide)),
        in_specs=[smem, smem, window_of(parts[1], columns, 0, 0),
                  window_of(ROWHALO, columns, seg // ROWHALO - 1, 0), vmem, vmem],
        out_specs=(vmem,) * 3,
    )(offsets, lengths, record, record, from_left, from_right)
    swap = [(i, i ^ 1) for i in range(shots) if i ^ 1 < shots]
    far, near = [None] * 4, [None] * 4
    second_last = shifted(mine, "shot", 2)
    top = shifted(wide_last, "shot", 1)
    bot = shifted(wide_first, "shot", -3)
    far[0] = shifted(first_part, "shot", -2)
    own = [first_part] + list(pl.pallas_call(
        functools.partial(widen_kernel, parts[1:4]),
        out_shape=tuple(part(k) for k in (1, 2, 3)),
        in_specs=[vmem, anywhere],
        out_specs=(vmem,) * 3,
    )(record, top))
    far[1] = shifted(own[1], "shot", -2)

    def pass_on(k, *others):
        ahead = [own[k + 2]] if k + 2 < 4 else []
        sent, *ahead = pl.pallas_call(
            functools.partial(pass_on_kernel, len(ahead) + len(others)),
            out_shape=(part(k),) + tuple(array(*x.shape) for x in ahead),
            in_specs=[anywhere] * (2 + len(ahead) + len(others)),
            out_specs=(vmem,) + (anywhere,) * len(ahead),
            input_output_aliases={2: 1} if ahead else {},
            scratch_shapes=[pltpu.SemaphoreType.DMA],
        )(own[k], far[k], *ahead, *others)
        near[k] = lax.ppermute(sent, "shot", swap)
        if ahead:
            own[k + 2] = ahead[0]
            far[k + 2] = shifted(own[k + 2], "shot", -2)
        return sent

    pass_on(0)

    def corner(row):
        return pl.BlockSpec((8, LANES), lambda _: (row // 8, 0))

    params = pl.pallas_call(
        shots_kernel,
        grid=(1,),
        out_shape=jax.ShapeDtypeStruct((8, LANES), jnp.int32),
        in_specs=[smem, corner(ROWHALO), smem, corner(HEAD), corner(HEAD)],
        out_specs=vmem,
    )(second_last, top, mine, near[0], far[0])
    pass_on(1, params, bot)

    into, back = ring_matrices(columns)
    work = pltpu.VMEM((PLANES, window + 4 * PAD, LANES), jnp.float32)

    def phase(out, arrays, pieces, halo_places, outers, span):
        held = [] if out is None else [out]
        return pl.pallas_call(
            functools.partial(
                deblend_kernel, (seg, columns), pieces, halo_places, outers, span, 2 + len(arrays) + len(held)
            ),
            out_shape=array(1, window, columns),
            in_specs=[smem, smem] + [anywhere] * (2 + len(arrays) + len(held)),
            out_specs=anywhere,
            input_output_aliases={} if out is None else {4 + len(arrays): 0},
            scratch_shapes=[
                pltpu.VMEM(into.shape, into.dtype),
                pltpu.VMEM(back.shape, back.dtype),
                pltpu.VMEM((3 * seg, columns), jnp.float32),
                pltpu.VMEM((3, HEAD, columns), jnp.float32),
                pltpu.VMEM((2, ROWHALO, wide), jnp.float32),
                pltpu.VMEM((2, PLANES, 3 * seg + 4 * PAD, LANES), jnp.float32),
                work, work, work,
                pltpu.VMEM((3, PLANES, STRIP + 32, LANES), jnp.float32),
                pltpu.VMEM((window + BLOCK, columns), jnp.float32),
                pltpu.SemaphoreType.DMA((len(pieces) + 7,)),
                pltpu.SemaphoreType.DMA((window // BLOCK,)),
            ],
            compiler_params=pltpu.CompilerParams(vmem_limit_bytes=60 * 1024 * 1024),
        )(params, thresholds, into, back, *arrays, *held)

    def part_piece(k, main, segment):
        return (main, skip if k == 0 else 0, parts[k + 1] - parts[k], segment * seg + parts[k])

    blocks = window // BLOCK
    cap = 9

    def mark(offset, rows):
        return jnp.clip((seg + rows - 28 - offset) // BLOCK, 0, blocks)

    def far_begin(offset):
        return jnp.minimum((2 * seg + 35 - offset) // 8 * 8 // BLOCK, blocks)

    def far_middle(offset):
        return jnp.clip((2 * seg + parts[2] - 28 - offset) // BLOCK, far_begin(offset), blocks)

    def takes_far(offset):
        return far_middle(offset) - far_begin(offset) >= 4

    def first(offset):
        is_far = takes_far(offset)
        begin = jnp.where(is_far, far_begin(offset), 0)
        return [(begin, jnp.where(is_far, far_middle(offset), jnp.minimum(mark(offset, 0), cap)))]

    def second(offset):
        is_far = takes_far(offset)
        begin = jnp.where(is_far, 0, first(offset)[0][1])
        return [(begin, mark(offset, parts[2])), (jnp.where(is_far, far_middle(offset), far_begin(offset)), blocks)]

    def last(offset):
        bridged = (jnp.minimum((2 * seg + 35 - offset) // 8 * 8, window) + BLOCK - 1) // BLOCK
        return [(mark(offset, parts[2]), bridged)]

    def every(places, segment):
        return [part_piece(k, place, segment) for k, place in enumerate(places)]

    out = phase(
        None, [*own, top, far[0], far[1]], every(range(4), 0) + every((5, 6), 2), (0, None, 5), [(4, -ROWHALO)], first
    )
    pass_on(2, out)
    sent = pass_on(3)
    out = phase(
        out, [*far, *own, near[0], near[1], bot, top, sent],
        every(range(4), 2) + every(range(4, 8), 0) + every((8, 9), 1), (4, 8, 0),
        [(10, 3 * seg), (11, -ROWHALO)], second,
    )
    return phase(
        out, [own[0], own[3], *near, far[0], far[1]],
        [part_piece(3, 1, 0)] + every(range(2, 6), 1) + every((6, 7), 2), (0, 2, 6), [], last,
    )


def solution(mesh):
    return jax.shard_map(
        on_device,
        mesh=mesh,
        in_specs=(P("shot", "rcv"), P("shot"), P("shot"), P()),
        out_specs=P("shot", None, "rcv"),
        check_vma=False,
    )
```

```python
import functools

import numpy as np
import jax
import jax.numpy as jnp
from jax import lax
from jax.experimental import pallas as pl
from jax.experimental.pallas import tpu as pltpu
from jax.sharding import PartitionSpec as P

LEVELS = 3
relax_step = 0.5

PLANES = 5
LANES = 128
RING = PLANES * LANES
HALF = LANES // 2
EDGE = 32
QUARTERS = LANES // EDGE
HEAD = 128
PAD = 64
ROWHALO = 16
BLOCK = 64
STRIP = 64


def shifted(shard, axis, by):
    devices = lax.axis_size(axis)
    pairs = [(i, i + by) for i in range(devices) if 0 <= i + by < devices]
    return lax.ppermute(shard, axis, pairs)


def ring_matrices(columns):
    wide = columns + 2 * LANES
    into = np.zeros((wide, RING), np.float32)
    back = np.zeros((RING, columns), np.float32)

    def place(ring):
        pair, side = divmod(ring, 2)
        return (pair % PLANES) * LANES + side * HALF + pair // PLANES

    for column in range(columns):
        into[column, place(EDGE + column)] = relax_step
        back[place(EDGE + column), column] = 1.0
    for quarter in range(LANES // EDGE):
        for i in range(EDGE):
            into[columns + quarter * EDGE + i, place(i)] = relax_step
            into[columns + LANES + quarter * EDGE + i, place(EDGE + columns + i)] = relax_step
    return jnp.asarray(into, jnp.bfloat16), jnp.asarray(back, jnp.bfloat16)


def smooth_across(planes, dilation):
    if dilation == 1:
        lane = lax.broadcasted_iota(jnp.int32, planes[0].shape, 1)
        other = [pltpu.roll(x, HALF, 1) for x in planes]
        before = [pltpu.roll(planes[-1], HALF + 1, 1)] + other[:-1]
        after = other[1:] + [pltpu.roll(planes[0], HALF - 1, 1)]
        two_before = [pltpu.roll(planes[-1], 1, 1)] + planes[:-1]
        two_after = planes[1:] + [pltpu.roll(planes[0], LANES - 1, 1)]
        return [
            (two_before[k] + two_after[k])
            + 4.0 * (other[k] + jnp.where(lane < HALF, before[k], after[k]))
            + 6.0 * planes[k]
            for k in range(PLANES)
        ]
    rolled = {}
    pairs = dilation // 2

    def at(position):
        turns, plane = divmod(position, PLANES)
        if turns == 0:
            return planes[plane]
        if (turns, plane) not in rolled:
            rolled[turns, plane] = pltpu.roll(planes[plane], (-turns) % LANES, 1)
        return rolled[turns, plane]

    return [
        (at(k - 2 * pairs) + at(k + 2 * pairs)) + 4.0 * (at(k - pairs) + at(k + pairs)) + 6.0 * planes[k]
        for k in range(PLANES)
    ]


def limit(values, cut):
    return jnp.minimum(jnp.maximum(values, -cut), cut)


def blocks_of(first, count, body):
    def step(b, carry):
        body(pl.multiple_of(first + b * (2 * BLOCK), 8), 2 * BLOCK)
        return carry

    lax.fori_loop(0, count // 2, step, 0)
    pl.when(count % 2 == 1)(lambda: body(pl.multiple_of(first + (count - 1) * BLOCK, 8), BLOCK))


def smooth_block(ref, start, rows, dilation, scale):
    centre, summed = [], []
    for k in range(PLANES):
        x = [ref[k, pl.ds(start + tap * dilation, rows), :] for tap in range(-2, 3)]
        centre.append(x[2])
        summed.append((x[0] + x[4]) + 4.0 * (x[1] + x[3]) + 6.0 * x[2])
    summed = smooth_across(summed, dilation)
    return centre, [s * w for s, w in zip(summed, scale)]


def deblend_kernel(geometry, pieces, halo_places, outers, span, operands, params, thr, *refs):
    seg, columns = geometry
    into_hbm, back_hbm, *sources = refs[:operands]
    out, into, back, ext, halos, beyond, gathered, c1, c2, f, strip, staged, sem, out_sem = refs[operands:]
    window = 2 * seg
    quarter_rows = seg // QUARTERS

    shots = lax.axis_size("shot")
    me = lax.axis_index("shot")
    rcv = lax.axis_index("rcv")
    offset = params[2, 0]
    live = params[2, 1]
    total = (shots - me) * seg - offset

    def shot(by):
        return by * seg + params[by + 2, 0] - offset, params[by + 2, 1]

    spans = [(pl.multiple_of(begin * BLOCK, 8), jnp.maximum(end - begin, 0)) for begin, end in span(offset)]
    some = sum(count for _, count in spans) > 0

    def reached(row, rows):
        found = False
        for low, count in spans:
            inside = (row < offset + low + count * BLOCK + 40) & (row + rows > offset + low - 40)
            found = found | ((count > 0) & inside)
        return found

    def copy_of(n, src, target):
        return pltpu.make_async_copy(src, target, sem.at[n])

    brought = [(0, None, into, some)]
    for main, first, rows, row in pieces:
        brought.append((main, (first, rows), ext.at[pl.ds(row, rows), :], reached(row, rows)))
    for segment, place in enumerate(halo_places):
        if place is not None:
            brought.append((place, (0, HEAD), halos.at[segment], some))
    for n, (place, row) in enumerate(outers):
        brought.append((place, (0, ROWHALO), beyond.at[n], reached(row, ROWHALO)))

    pl.when(some)(lambda: copy_of(0, into_hbm, into).start())
    for n, (place, part, target, wanted) in enumerate(brought):
        if part is not None:
            pl.when(wanted)(lambda: copy_of(n, sources[place].at[pl.ds(*part), :], target).start())
    pl.when(some)(lambda: copy_of(len(brought), back_hbm, back).start())

    lane = lax.broadcasted_iota(jnp.int32, (1, LANES), 1)
    has_right = jnp.where(rcv < lax.axis_size("rcv") - 1, 1.0, 0.0)
    has_left = jnp.where(rcv > 0, 1.0, 0.0)
    scale = []
    for k in range(PLANES):
        ring = 2 * (lane % HALF * PLANES + k) + lane // HALF
        side = jnp.where(ring < EDGE, has_left, has_right)
        scale.append(jnp.where((ring >= EDGE) & (ring < EDGE + columns), 1.0, side) * (1.0 / 256.0))
    strip[:, :, 0:16, :] = jnp.zeros((3, PLANES, 16, LANES), jnp.float32)
    strip[:, :, 16 + STRIP : 32 + STRIP, :] = jnp.zeros((3, PLANES, 16, LANES), jnp.float32)

    for n, (place, part, target, wanted) in enumerate(brought):
        pl.when(wanted)(lambda: copy_of(n, target, target).wait())

    def permute_in(main, left, right, quarter, row):
        mine = (lane // EDGE) == quarter
        lhs = [main] + [jnp.where(mine, x, 0.0) for x in (left, right)]
        lhs = jnp.concatenate([x.astype(jnp.bfloat16) for x in lhs], axis=1)
        result = jnp.dot(lhs, into[...], preferred_element_type=jnp.float32)
        for k in range(PLANES):
            gathered[0, k, pl.ds(PAD + row, main.shape[0]), :] = result[:, k * LANES : (k + 1) * LANES]

    def permute_quarter(i, carry):
        row = pl.multiple_of(i * quarter_rows, quarter_rows)
        segment = row // seg
        sides = []
        for side in range(2):
            lanes = [2 * side * LANES + at // HEAD * LANES for at in range(0, quarter_rows, HEAD)]
            sides.append(jnp.concatenate([halos[segment, :, at : at + LANES] for at in lanes], axis=0))
        permute_in(ext[pl.ds(row, quarter_rows), :], *sides, lax.rem(row, seg) // quarter_rows, row)
        return carry

    for low, count in spans:
        begin = jnp.clip((offset + low - 40) // quarter_rows, 0, 3 * QUARTERS)
        end = jnp.clip((offset + low + count * BLOCK + 40 + quarter_rows - 1) // quarter_rows, 0, 3 * QUARTERS)
        lax.fori_loop(begin, jnp.where(count > 0, end, begin), permute_quarter, 0)
    for n, (place, row) in enumerate(outers):

        @pl.when(reached(row, ROWHALO))
        def _():
            sides = [beyond[n, :, columns + side * LANES : columns + (side + 1) * LANES] for side in range(2)]
            permute_in(beyond[n, :, 0:columns], *sides, QUARTERS - 1 if row < 0 else 0, row)

    def level_pass(source, shift, target, dilation, first, count):
        def body(at, rows):
            _, summed = smooth_block(source, at + shift, rows, dilation, scale)
            for k in range(PLANES):
                target[k, pl.ds(at, rows), :] = summed[k]

        blocks_of(first, count, body)

    def shrunk(sweep, shift, at, rows):
        centre, summed = smooth_block(c2, at, rows, 4, scale)
        for k in range(PLANES):
            x0 = gathered[sweep, k, pl.ds(at + shift, rows), :]
            x1 = c1[k, pl.ds(at, rows), :]
            x2 = centre[k]
            clipped = limit(x0 - x1, thr[0]) + limit(x1 - x2, thr[1]) + limit(x2 - summed[k], thr[2])
            yield k, x0, x0 - clipped

    def next_gathered(at, rows):
        t = at - PAD + lax.broadcasted_iota(jnp.int32, (rows, LANES), 0)
        shots_live = jnp.zeros(t.shape, jnp.float32)
        for by in range(-2, 3):
            begin, length = shot(by)
            shots_live = shots_live + jnp.where((t >= begin) & (t < begin + length), 1.0, 0.0)
        own_live = jnp.where((t >= 0) & (t < live), 1.0, 0.0)
        inside = jnp.where(t < total, relax_step, 0.0)
        factor = own_live * (1.0 - inside * shots_live)
        for k, x0, value in shrunk(0, offset, at, rows):
            f[k, pl.ds(at, rows), :] = value
            gathered[1, k, pl.ds(at, rows), :] = own_live * x0 + factor * value

    half = STRIP // 2

    def do_strip(by, at_end):
        begin, length = shot(by)
        p = begin + jnp.where(at_end, length, 0)
        t = p - half + lax.broadcasted_iota(jnp.int32, (STRIP, LANES), 0)
        in_live = jnp.where((t >= begin) & (t < begin + length), 1.0, 0.0)
        in_window = jnp.where((t >= begin) & (t < begin + window), 1.0, 0.0)
        for k in range(PLANES):
            strip[0, k, 16 : 16 + STRIP, :] = gathered[0, k, pl.ds(PAD + offset + p - half, STRIP), :] * in_live
        for j in range(2):
            _, summed = smooth_block(strip.at[j], 16, STRIP, 2**j, scale)
            for k in range(PLANES):
                strip[j + 1, k, 16 : 16 + STRIP, :] = summed[k] * in_window
        mid = half
        _, summed = smooth_block(strip.at[2], mid, 32, 4, scale)
        t = p - 16 + lax.broadcasted_iota(jnp.int32, (32, LANES), 0)
        in_window = jnp.where((t >= begin) & (t < begin + window), 1.0, 0.0)
        near_edge = (t >= begin) & (t < begin + length) & (t >= p - 14) & (t < p + 14)
        own_live = (t >= 0) & (t < live)
        inside = jnp.where(t < total, -relax_step, 0.0)
        weight = jnp.where(near_edge & own_live, inside + jnp.where(by == 0, 1.0, 0.0), 0.0)
        for k in range(PLANES):
            x0 = strip[0, k, mid : mid + 32, :]
            x1 = strip[1, k, mid : mid + 32, :]
            x2 = strip[2, k, mid : mid + 32, :]
            x3 = summed[k] * in_window
            clipped = limit(x0 - x1, thr[0]) + limit(x1 - x2, thr[1]) + limit(x2 - x3, thr[2])
            where = pl.ds(PAD + p - 16, 32)
            gathered[1, k, where, :] = gathered[1, k, where, :] + weight * (x0 - clipped - f[k, where, :])

    def out_copy(block):
        rows = pl.ds(pl.multiple_of(block * BLOCK, BLOCK), BLOCK)
        return pltpu.make_async_copy(staged.at[rows, :], out.at[0, rows, :], out_sem.at[block])

    def estimate(at, rows):
        t = at - PAD + lax.broadcasted_iota(jnp.int32, (rows, LANES), 0)
        own_live = jnp.where(t < live, 1.0, 0.0)
        high, rest = [], []
        for k, _, value in shrunk(1, 0, at, rows):
            x = own_live * value
            h = x.astype(jnp.bfloat16)
            high.append(h)
            rest.append((x - h.astype(jnp.float32)).astype(jnp.bfloat16))
        both = jnp.concatenate([jnp.concatenate(high, axis=1), jnp.concatenate(rest, axis=1)], axis=0)
        result = jnp.dot(both, back[...], preferred_element_type=jnp.float32)
        staged[pl.ds(pl.multiple_of(at - PAD, 8), rows), :] = result[:rows] + result[rows:]
        for n in range(rows // BLOCK):
            out_copy((at - PAD) // BLOCK + n).start()

    def clear_edges(ref):
        ref[:, PAD - 16 : PAD, :] = jnp.zeros((PLANES, 16, LANES), jnp.float32)
        ref[:, PAD + window : PAD + window + 16, :] = jnp.zeros((PLANES, 16, LANES), jnp.float32)

    def process(low, count):
        high = low + count * BLOCK
        first = PAD + low
        wider, many = first - BLOCK // 2, count + 1

        def strip_step(i, carry):
            by, at_end = i // 2 - 2, i % 2 == 1
            begin, length = shot(by)
            p = begin + jnp.where(at_end, length, 0)
            begins_at = jnp.where(at_end, p - 14, p)
            bottom = jnp.maximum(low - 14, 0)
            top = jnp.minimum(high + 14, live)

            @pl.when((length > 0) & (begins_at + 14 > bottom) & (begins_at < top))
            def _():
                do_strip(by, at_end)

            return carry

        level_pass(gathered.at[0], offset, c1, 1, wider, many)
        level_pass(c1, 0, c2, 2, wider, many)
        blocks_of(wider, many, next_gathered)
        lax.fori_loop(1, 10, strip_step, 0)
        clear_edges(gathered.at[1])
        level_pass(gathered.at[1], 0, c1, 1, wider, many)
        clear_edges(c1)
        level_pass(c1, 0, c2, 2, wider, many)
        clear_edges(c2)
        blocks_of(first, count, estimate)

    pl.when(some)(lambda: copy_of(len(brought), back, back).wait())

    def span_step(i, carry):
        low, count = spans[0]
        if len(spans) > 1:
            low, count = jnp.where(i == 0, low, spans[1][0]), jnp.where(i == 0, count, spans[1][1])
        pl.when(count > 0)(lambda: process(pl.multiple_of(low, 8), count))
        return carry

    lax.fori_loop(0, len(spans), span_step, 0)

    def wait(i, carry):
        out_copy(i).wait()
        return carry

    for low, count in spans:
        lax.fori_loop(low // BLOCK, low // BLOCK + count, wait, 0)


def prepare_kernel(first_columns, last_columns, first_edge, last_edge):
    quarter = first_edge.shape[0]
    lane = lax.broadcasted_iota(jnp.int32, (1, LANES), 1)
    for out, source, inner in ((first_edge, first_columns, 0), (last_edge, last_columns, LANES - EDGE)):
        packed = jnp.zeros((quarter, LANES), jnp.float32)
        for q in range(QUARTERS):
            rows = source[q * quarter : (q + 1) * quarter, :].astype(jnp.float32)
            turn = (q * EDGE - inner) % LANES
            packed = jnp.where(lane // EDGE == q, pltpu.roll(rows, turn, 1) if turn else rows, packed)
        out[...] = packed


def header_kernel(offsets, lengths, first_rows, last_rows, left, right, own, wide_first, wide_last):
    quarter = left.shape[0]
    columns = own.shape[1]
    lane = lax.broadcasted_iota(jnp.int32, (8, LANES), 1)
    about = jnp.where(lane == 0, offsets[0], jnp.where(lane == 1, lengths[0], 0)).astype(jnp.float32)
    for side, halo in enumerate((left, right)):
        for part in range(quarter // HEAD):
            at = (2 * side + part) * LANES
            own[0:HEAD, at : at + LANES] = halo[part * HEAD : (part + 1) * HEAD, :]
    own[HEAD : HEAD + 8, :] = jnp.concatenate([about] * (columns // LANES), axis=1)
    own[HEAD + 8 :, :] = first_rows[...].astype(jnp.float32)
    wide_first[:, 0:columns] = first_rows[0:ROWHALO, :].astype(jnp.float32)
    wide_last[0:ROWHALO, 0:columns] = last_rows[...].astype(jnp.float32)
    for side, halo in enumerate((left, right)):
        at = columns + side * LANES
        wide_first[:, at : at + LANES] = halo[0:ROWHALO, :]
        wide_last[0:ROWHALO, at : at + LANES] = halo[quarter - ROWHALO : quarter, :]
    wide_last[ROWHALO:, :] = jnp.concatenate([about] * (columns // LANES + 2), axis=1)


def widen_kernel(begins, record, wait, *own):
    for begin, out in zip(begins, own):
        out[...] = record[begin : begin + out.shape[0], :].astype(jnp.float32)


def pass_on_kernel(unread, own, far, *refs):
    sent, sem = refs[unread], refs[-1]
    odd = lax.rem(lax.axis_index("shot"), 2) == 1
    pl.when(odd)(lambda: pltpu.make_async_copy(own, sent, sem).start())
    pl.when(jnp.logical_not(odd))(lambda: pltpu.make_async_copy(far, sent, sem).start())
    pltpu.make_async_copy(own, sent, sem).wait()


def shots_kernel(second_last, last, mine, following, second, out):
    lane = lax.broadcasted_iota(jnp.int32, (8, LANES), 1)
    row = lax.broadcasted_iota(jnp.int32, (8, LANES), 0)
    found = jnp.zeros((8, LANES), jnp.float32)
    for n, pair in enumerate((second_last, last, mine, following, second)):
        if n in (0, 2):
            value = jnp.where(lane == 0, pair[0], pair[1])
        else:
            value = pair[0:1, :]
        found = jnp.where(row == n, value, found)
    out[...] = found.astype(jnp.int32)


def on_device(record, offsets, lengths, thresholds):
    seg, columns = record.shape
    window = 2 * seg
    shots = lax.axis_size("shot")
    q = seg // QUARTERS
    skip = HEAD + 8
    step = (seg + skip + 4 * 16 - 1) // (4 * 16) * 16
    parts = [0] + [seg - k * step for k in (3, 2, 1, 0)]
    swap = [(i, i ^ 1) for i in range(shots) if i ^ 1 < shots]
    smem = pl.BlockSpec(memory_space=pltpu.SMEM)
    anywhere = pl.BlockSpec(memory_space=pl.ANY)
    vmem = pl.BlockSpec(memory_space=pltpu.VMEM)

    def array(*shape):
        return jax.ShapeDtypeStruct(shape, jnp.float32)

    def part(k):
        return array(parts[k + 1] - parts[k] + (skip if k == 0 else 0), columns)

    def window_of(rows, width, row, column):
        return pl.BlockSpec((rows, width), lambda _: (row, column))

    first_edge, last_edge = pl.pallas_call(
        prepare_kernel,
        grid=(1,),
        out_shape=(array(q, LANES), array(q, LANES)),
        in_specs=[window_of(seg, LANES, 0, 0), window_of(seg, LANES, 0, columns // LANES - 1)],
        out_specs=(vmem, vmem),
    )(record, record)
    from_left = shifted(last_edge, "rcv", 1)
    from_right = shifted(first_edge, "rcv", -1)
    mine = jnp.concatenate([offsets, lengths]).astype(jnp.float32)
    wide = columns + 2 * LANES
    first_part, wide_first, wide_last = pl.pallas_call(
        header_kernel,
        grid=(1,),
        out_shape=(part(0), array(ROWHALO, wide), array(ROWHALO + 8, wide)),
        in_specs=[smem, smem, window_of(parts[1], columns, 0, 0),
                  window_of(ROWHALO, columns, seg // ROWHALO - 1, 0), vmem, vmem],
        out_specs=(vmem,) * 3,
    )(offsets, lengths, record, record, from_left, from_right)
    swap = [(i, i ^ 1) for i in range(shots) if i ^ 1 < shots]
    far, near = [None] * 4, [None] * 4
    second_last = shifted(mine, "shot", 2)
    top = shifted(wide_last, "shot", 1)
    bot = shifted(wide_first, "shot", -3)
    far[0] = shifted(first_part, "shot", -2)
    own = [first_part] + list(pl.pallas_call(
        functools.partial(widen_kernel, parts[1:4]),
        out_shape=tuple(part(k) for k in (1, 2, 3)),
        in_specs=[vmem, anywhere],
        out_specs=(vmem,) * 3,
    )(record, top))
    far[1] = shifted(own[1], "shot", -2)

    def pass_on(k, *others):
        ahead = [own[k + 2]] if k + 2 < 4 else []
        sent, *ahead = pl.pallas_call(
            functools.partial(pass_on_kernel, len(ahead) + len(others)),
            out_shape=(part(k),) + tuple(array(*x.shape) for x in ahead),
            in_specs=[anywhere] * (2 + len(ahead) + len(others)),
            out_specs=(vmem,) + (anywhere,) * len(ahead),
            input_output_aliases={2: 1} if ahead else {},
            scratch_shapes=[pltpu.SemaphoreType.DMA],
        )(own[k], far[k], *ahead, *others)
        near[k] = lax.ppermute(sent, "shot", swap)
        if ahead:
            own[k + 2] = ahead[0]
            far[k + 2] = shifted(own[k + 2], "shot", -2)
        return sent

    pass_on(0)

    def corner(row):
        return pl.BlockSpec((8, LANES), lambda _: (row // 8, 0))

    params = pl.pallas_call(
        shots_kernel,
        grid=(1,),
        out_shape=jax.ShapeDtypeStruct((8, LANES), jnp.int32),
        in_specs=[smem, corner(ROWHALO), smem, corner(HEAD), corner(HEAD)],
        out_specs=vmem,
    )(second_last, top, mine, near[0], far[0])
    pass_on(1, params, bot)

    into, back = ring_matrices(columns)
    work = pltpu.VMEM((PLANES, window + 4 * PAD, LANES), jnp.float32)

    def phase(out, arrays, pieces, halo_places, outers, span):
        held = [] if out is None else [out]
        return pl.pallas_call(
            functools.partial(
                deblend_kernel, (seg, columns), pieces, halo_places, outers, span, 2 + len(arrays) + len(held)
            ),
            out_shape=array(1, window, columns),
            in_specs=[smem, smem] + [anywhere] * (2 + len(arrays) + len(held)),
            out_specs=anywhere,
            input_output_aliases={} if out is None else {4 + len(arrays): 0},
            scratch_shapes=[
                pltpu.VMEM(into.shape, into.dtype),
                pltpu.VMEM(back.shape, back.dtype),
                pltpu.VMEM((3 * seg, columns), jnp.float32),
                pltpu.VMEM((3, HEAD, columns), jnp.float32),
                pltpu.VMEM((2, ROWHALO, wide), jnp.float32),
                pltpu.VMEM((2, PLANES, 3 * seg + 4 * PAD, LANES), jnp.float32),
                work, work, work,
                pltpu.VMEM((3, PLANES, STRIP + 32, LANES), jnp.float32),
                pltpu.VMEM((window + BLOCK, columns), jnp.float32),
                pltpu.SemaphoreType.DMA((len(pieces) + 7,)),
                pltpu.SemaphoreType.DMA((window // BLOCK,)),
            ],
            compiler_params=pltpu.CompilerParams(vmem_limit_bytes=63 * 1024 * 1024),
        )(params, thresholds, into, back, *arrays, *held)

    def part_piece(k, main, segment):
        return (main, skip if k == 0 else 0, parts[k + 1] - parts[k], segment * seg + parts[k])

    blocks = window // BLOCK
    cap = 9

    def mark(offset, rows):
        return jnp.clip((seg + rows - 28 - offset) // BLOCK, 0, blocks)

    def far_begin(offset):
        return jnp.minimum((2 * seg + 35 - offset) // 8 * 8 // BLOCK, blocks)

    def far_middle(offset):
        return jnp.clip((2 * seg + parts[2] - 28 - offset) // BLOCK, far_begin(offset), blocks)

    def takes_far(offset):
        return far_middle(offset) - far_begin(offset) >= 4

    def first(offset):
        is_far = takes_far(offset)
        begin = jnp.where(is_far, far_begin(offset), 0)
        return [(begin, jnp.where(is_far, far_middle(offset), jnp.minimum(mark(offset, 0), cap)))]

    def second(offset):
        is_far = takes_far(offset)
        begin = jnp.where(is_far, 0, first(offset)[0][1])
        return [(begin, mark(offset, parts[2])), (jnp.where(is_far, far_middle(offset), far_begin(offset)), blocks)]

    def last(offset):
        bridged = (jnp.minimum((2 * seg + 35 - offset) // 8 * 8, window) + BLOCK - 1) // BLOCK
        return [(mark(offset, parts[2]), bridged)]

    def every(places, segment):
        return [part_piece(k, place, segment) for k, place in enumerate(places)]

    out = phase(
        None, [*own, top, far[0], far[1]], every(range(4), 0) + every((5, 6), 2), (0, None, 5), [(4, -ROWHALO)], first
    )
    pass_on(2, out)
    sent = pass_on(3)
    out = phase(
        out, [*far, *own, near[0], near[1], bot, top, sent],
        every(range(4), 2) + every(range(4, 8), 0) + every((8, 9), 1), (4, 8, 0),
        [(10, 3 * seg), (11, -ROWHALO)], second,
    )
    return phase(
        out, [own[0], own[3], *near, far[0], far[1]],
        [part_piece(3, 1, 0)] + every(range(2, 6), 1) + every((6, 7), 2), (0, 2, 6), [], last,
    )


def solution(mesh):
    return jax.shard_map(
        on_device,
        mesh=mesh,
        in_specs=(P("shot", "rcv"), P("shot"), P("shot"), P()),
        out_specs=P("shot", None, "rcv"),
        check_vma=False,
    )
```

```python
import functools

import numpy as np
import jax
import jax.numpy as jnp
from jax import lax
from jax.experimental import pallas as pl
from jax.experimental.pallas import tpu as pltpu
from jax.sharding import PartitionSpec as P

LEVELS = 3
relax_step = 0.5

PLANES = 5
LANES = 128
RING = PLANES * LANES
HALF = LANES // 2
EDGE = 32
QUARTERS = LANES // EDGE
HEAD = 128
PAD = 64
ROWHALO = 16
BLOCK = 64
STRIP = 64


def shifted(shard, axis, by):
    devices = lax.axis_size(axis)
    pairs = [(i, i + by) for i in range(devices) if 0 <= i + by < devices]
    return lax.ppermute(shard, axis, pairs)


def ring_matrices(columns):
    wide = columns + 2 * LANES
    into = np.zeros((wide, RING), np.float32)
    back = np.zeros((RING, columns), np.float32)

    def place(ring):
        pair, side = divmod(ring, 2)
        return (pair % PLANES) * LANES + side * HALF + pair // PLANES

    for column in range(columns):
        into[column, place(EDGE + column)] = relax_step
        back[place(EDGE + column), column] = 1.0
    for quarter in range(LANES // EDGE):
        for i in range(EDGE):
            into[columns + quarter * EDGE + i, place(i)] = relax_step
            into[columns + LANES + quarter * EDGE + i, place(EDGE + columns + i)] = relax_step
    return jnp.asarray(into, jnp.bfloat16), jnp.asarray(back, jnp.bfloat16)


def smooth_across(planes, dilation):
    if dilation == 1:
        lane = lax.broadcasted_iota(jnp.int32, planes[0].shape, 1)
        other = [pltpu.roll(x, HALF, 1) for x in planes]
        before = [pltpu.roll(planes[-1], HALF + 1, 1)] + other[:-1]
        after = other[1:] + [pltpu.roll(planes[0], HALF - 1, 1)]
        two_before = [pltpu.roll(planes[-1], 1, 1)] + planes[:-1]
        two_after = planes[1:] + [pltpu.roll(planes[0], LANES - 1, 1)]
        return [
            (two_before[k] + two_after[k])
            + 4.0 * (other[k] + jnp.where(lane < HALF, before[k], after[k]))
            + 6.0 * planes[k]
            for k in range(PLANES)
        ]
    rolled = {}
    pairs = dilation // 2

    def at(position):
        turns, plane = divmod(position, PLANES)
        if turns == 0:
            return planes[plane]
        if (turns, plane) not in rolled:
            rolled[turns, plane] = pltpu.roll(planes[plane], (-turns) % LANES, 1)
        return rolled[turns, plane]

    return [
        (at(k - 2 * pairs) + at(k + 2 * pairs)) + 4.0 * (at(k - pairs) + at(k + pairs)) + 6.0 * planes[k]
        for k in range(PLANES)
    ]


def limit(values, cut):
    return jnp.minimum(jnp.maximum(values, -cut), cut)


def blocks_of(first, count, body):
    def step(b, carry):
        body(pl.multiple_of(first + b * (2 * BLOCK), 8), 2 * BLOCK)
        return carry

    lax.fori_loop(0, count // 2, step, 0)
    pl.when(count % 2 == 1)(lambda: body(pl.multiple_of(first + (count - 1) * BLOCK, 8), BLOCK))


def smooth_block(ref, start, rows, dilation, scale):
    centre, summed = [], []
    for k in range(PLANES):
        x = [ref[k, pl.ds(start + tap * dilation, rows), :] for tap in range(-2, 3)]
        centre.append(x[2])
        summed.append((x[0] + x[4]) + 4.0 * (x[1] + x[3]) + 6.0 * x[2])
    summed = smooth_across(summed, dilation)
    return centre, [s * w for s, w in zip(summed, scale)]


def deblend_kernel(geometry, pieces, halo_places, outers, span, operands, params, thr, *refs):
    seg, columns = geometry
    into_hbm, back_hbm, *sources = refs[:operands]
    out, into, back, ext, halos, beyond, gathered, c1, c2, f, strip, staged, sem, out_sem = refs[operands:]
    window = 2 * seg
    quarter_rows = seg // QUARTERS

    shots = lax.axis_size("shot")
    me = lax.axis_index("shot")
    rcv = lax.axis_index("rcv")
    offset = params[2, 0]
    live = params[2, 1]
    total = (shots - me) * seg - offset

    def shot(by):
        return by * seg + params[by + 2, 0] - offset, params[by + 2, 1]

    spans = [(pl.multiple_of(begin * BLOCK, 8), jnp.maximum(end - begin, 0)) for begin, end in span(offset)]
    some = sum(count for _, count in spans) > 0

    def reached(row, rows):
        found = False
        for low, count in spans:
            inside = (row < offset + low + count * BLOCK + 40) & (row + rows > offset + low - 40)
            found = found | ((count > 0) & inside)
        return found

    def copy_of(n, src, target):
        return pltpu.make_async_copy(src, target, sem.at[n])

    brought = [(0, None, into, some)]
    for main, first, rows, row in pieces:
        brought.append((main, (first, rows), ext.at[pl.ds(row, rows), :], reached(row, rows)))
    for segment, place in enumerate(halo_places):
        if place is not None:
            brought.append((place, (0, HEAD), halos.at[segment], some))
    for n, (place, row) in enumerate(outers):
        brought.append((place, (0, ROWHALO), beyond.at[n], reached(row, ROWHALO)))

    pl.when(some)(lambda: copy_of(0, into_hbm, into).start())
    for n, (place, part, target, wanted) in enumerate(brought):
        if part is not None:
            pl.when(wanted)(lambda: copy_of(n, sources[place].at[pl.ds(*part), :], target).start())
    pl.when(some)(lambda: copy_of(len(brought), back_hbm, back).start())

    lane = lax.broadcasted_iota(jnp.int32, (1, LANES), 1)
    has_right = jnp.where(rcv < lax.axis_size("rcv") - 1, 1.0, 0.0)
    has_left = jnp.where(rcv > 0, 1.0, 0.0)
    scale = []
    for k in range(PLANES):
        ring = 2 * (lane % HALF * PLANES + k) + lane // HALF
        side = jnp.where(ring < EDGE, has_left, has_right)
        scale.append(jnp.where((ring >= EDGE) & (ring < EDGE + columns), 1.0, side) * (1.0 / 256.0))
    strip[:, :, 0:16, :] = jnp.zeros((3, PLANES, 16, LANES), jnp.float32)
    strip[:, :, 16 + STRIP : 32 + STRIP, :] = jnp.zeros((3, PLANES, 16, LANES), jnp.float32)

    for n, (place, part, target, wanted) in enumerate(brought):
        pl.when(wanted)(lambda: copy_of(n, target, target).wait())

    def permute_in(main, left, right, quarter, row):
        mine = (lane // EDGE) == quarter
        lhs = [main] + [jnp.where(mine, x, 0.0) for x in (left, right)]
        lhs = jnp.concatenate([x.astype(jnp.bfloat16) for x in lhs], axis=1)
        result = jnp.dot(lhs, into[...], preferred_element_type=jnp.float32)
        for k in range(PLANES):
            gathered[0, k, pl.ds(PAD + row, main.shape[0]), :] = result[:, k * LANES : (k + 1) * LANES]

    def permute_quarter(i, carry):
        row = pl.multiple_of(i * quarter_rows, quarter_rows)
        segment = row // seg
        sides = []
        for side in range(2):
            lanes = [2 * side * LANES + at // HEAD * LANES for at in range(0, quarter_rows, HEAD)]
            sides.append(jnp.concatenate([halos[segment, :, at : at + LANES] for at in lanes], axis=0))
        permute_in(ext[pl.ds(row, quarter_rows), :], *sides, lax.rem(row, seg) // quarter_rows, row)
        return carry

    for low, count in spans:
        begin = jnp.clip((offset + low - 40) // quarter_rows, 0, 3 * QUARTERS)
        end = jnp.clip((offset + low + count * BLOCK + 40 + quarter_rows - 1) // quarter_rows, 0, 3 * QUARTERS)
        lax.fori_loop(begin, jnp.where(count > 0, end, begin), permute_quarter, 0)
    for n, (place, row) in enumerate(outers):

        @pl.when(reached(row, ROWHALO))
        def _():
            sides = [beyond[n, :, columns + side * LANES : columns + (side + 1) * LANES] for side in range(2)]
            permute_in(beyond[n, :, 0:columns], *sides, QUARTERS - 1 if row < 0 else 0, row)

    def level_pass(source, shift, target, dilation, first, count):
        def body(at, rows):
            _, summed = smooth_block(source, at + shift, rows, dilation, scale)
            for k in range(PLANES):
                target[k, pl.ds(at, rows), :] = summed[k]

        blocks_of(first, count, body)

    def shrunk(sweep, shift, at, rows):
        centre, summed = smooth_block(c2, at, rows, 4, scale)
        for k in range(PLANES):
            x0 = gathered[sweep, k, pl.ds(at + shift, rows), :]
            x1 = c1[k, pl.ds(at, rows), :]
            x2 = centre[k]
            clipped = limit(x0 - x1, thr[0]) + limit(x1 - x2, thr[1]) + limit(x2 - summed[k], thr[2])
            yield k, x0, x0 - clipped

    def next_gathered(at, rows):
        t = at - PAD + lax.broadcasted_iota(jnp.int32, (rows, LANES), 0)
        shots_live = jnp.zeros(t.shape, jnp.float32)
        for by in range(-2, 3):
            begin, length = shot(by)
            shots_live = shots_live + jnp.where((t >= begin) & (t < begin + length), 1.0, 0.0)
        own_live = jnp.where((t >= 0) & (t < live), 1.0, 0.0)
        inside = jnp.where(t < total, relax_step, 0.0)
        factor = own_live * (1.0 - inside * shots_live)
        for k, x0, value in shrunk(0, offset, at, rows):
            f[k, pl.ds(at, rows), :] = value
            gathered[1, k, pl.ds(at, rows), :] = own_live * x0 + factor * value

    half = STRIP // 2

    def do_strip(by, at_end):
        begin, length = shot(by)
        p = begin + jnp.where(at_end, length, 0)
        t = p - half + lax.broadcasted_iota(jnp.int32, (STRIP, LANES), 0)
        in_live = jnp.where((t >= begin) & (t < begin + length), 1.0, 0.0)
        in_window = jnp.where((t >= begin) & (t < begin + window), 1.0, 0.0)
        for k in range(PLANES):
            strip[0, k, 16 : 16 + STRIP, :] = gathered[0, k, pl.ds(PAD + offset + p - half, STRIP), :] * in_live
        for j in range(2):
            _, summed = smooth_block(strip.at[j], 16, STRIP, 2**j, scale)
            for k in range(PLANES):
                strip[j + 1, k, 16 : 16 + STRIP, :] = summed[k] * in_window
        mid = half
        _, summed = smooth_block(strip.at[2], mid, 32, 4, scale)
        t = p - 16 + lax.broadcasted_iota(jnp.int32, (32, LANES), 0)
        in_window = jnp.where((t >= begin) & (t < begin + window), 1.0, 0.0)
        near_edge = (t >= begin) & (t < begin + length) & (t >= p - 14) & (t < p + 14)
        own_live = (t >= 0) & (t < live)
        inside = jnp.where(t < total, -relax_step, 0.0)
        weight = jnp.where(near_edge & own_live, inside + jnp.where(by == 0, 1.0, 0.0), 0.0)
        for k in range(PLANES):
            x0 = strip[0, k, mid : mid + 32, :]
            x1 = strip[1, k, mid : mid + 32, :]
            x2 = strip[2, k, mid : mid + 32, :]
            x3 = summed[k] * in_window
            clipped = limit(x0 - x1, thr[0]) + limit(x1 - x2, thr[1]) + limit(x2 - x3, thr[2])
            where = pl.ds(PAD + p - 16, 32)
            gathered[1, k, where, :] = gathered[1, k, where, :] + weight * (x0 - clipped - f[k, where, :])

    def out_copy(block):
        rows = pl.ds(pl.multiple_of(block * BLOCK, BLOCK), BLOCK)
        return pltpu.make_async_copy(staged.at[rows, :], out.at[0, rows, :], out_sem.at[block])

    def estimate(at, rows):
        t = at - PAD + lax.broadcasted_iota(jnp.int32, (rows, LANES), 0)
        own_live = jnp.where(t < live, 1.0, 0.0)
        high, rest = [], []
        for k, _, value in shrunk(1, 0, at, rows):
            x = own_live * value
            h = x.astype(jnp.bfloat16)
            high.append(h)
            rest.append((x - h.astype(jnp.float32)).astype(jnp.bfloat16))
        both = jnp.concatenate([jnp.concatenate(high, axis=1), jnp.concatenate(rest, axis=1)], axis=0)
        result = jnp.dot(both, back[...], preferred_element_type=jnp.float32)
        staged[pl.ds(pl.multiple_of(at - PAD, 8), rows), :] = result[:rows] + result[rows:]
        for n in range(rows // BLOCK):
            out_copy((at - PAD) // BLOCK + n).start()

    def clear_edges(ref):
        ref[:, PAD - 16 : PAD, :] = jnp.zeros((PLANES, 16, LANES), jnp.float32)
        ref[:, PAD + window : PAD + window + 16, :] = jnp.zeros((PLANES, 16, LANES), jnp.float32)

    def process(low, count):
        high = low + count * BLOCK
        first = PAD + low
        wider, many = first - BLOCK // 2, count + 1

        def strip_step(i, carry):
            by, at_end = i // 2 - 2, i % 2 == 1
            begin, length = shot(by)
            p = begin + jnp.where(at_end, length, 0)
            begins_at = jnp.where(at_end, p - 14, p)
            bottom = jnp.maximum(low - 14, 0)
            top = jnp.minimum(high + 14, live)

            @pl.when((length > 0) & (begins_at + 14 > bottom) & (begins_at < top))
            def _():
                do_strip(by, at_end)

            return carry

        level_pass(gathered.at[0], offset, c1, 1, wider, many)
        level_pass(c1, 0, c2, 2, wider, many)
        blocks_of(wider, many, next_gathered)
        lax.fori_loop(1, 10, strip_step, 0)
        clear_edges(gathered.at[1])
        level_pass(gathered.at[1], 0, c1, 1, wider, many)
        clear_edges(c1)
        level_pass(c1, 0, c2, 2, wider, many)
        clear_edges(c2)
        blocks_of(first, count, estimate)

    pl.when(some)(lambda: copy_of(len(brought), back, back).wait())

    def span_step(i, carry):
        low, count = spans[0]
        if len(spans) > 1:
            low, count = jnp.where(i == 0, low, spans[1][0]), jnp.where(i == 0, count, spans[1][1])
        pl.when(count > 0)(lambda: process(pl.multiple_of(low, 8), count))
        return carry

    lax.fori_loop(0, len(spans), span_step, 0)

    def wait(i, carry):
        out_copy(i).wait()
        return carry

    for low, count in spans:
        lax.fori_loop(low // BLOCK, low // BLOCK + count, wait, 0)


def prepare_kernel(first_columns, last_columns, first_edge, last_edge):
    quarter = first_edge.shape[0]
    lane = lax.broadcasted_iota(jnp.int32, (1, LANES), 1)
    for out, source, inner in ((first_edge, first_columns, 0), (last_edge, last_columns, LANES - EDGE)):
        packed = jnp.zeros((quarter, LANES), jnp.float32)
        for q in range(QUARTERS):
            rows = source[q * quarter : (q + 1) * quarter, :].astype(jnp.float32)
            turn = (q * EDGE - inner) % LANES
            packed = jnp.where(lane // EDGE == q, pltpu.roll(rows, turn, 1) if turn else rows, packed)
        out[...] = packed


def header_kernel(offsets, lengths, first_rows, last_rows, left, right, own, wide_first, wide_last):
    quarter = left.shape[0]
    columns = own.shape[1]
    lane = lax.broadcasted_iota(jnp.int32, (8, LANES), 1)
    about = jnp.where(lane == 0, offsets[0], jnp.where(lane == 1, lengths[0], 0)).astype(jnp.float32)
    for side, halo in enumerate((left, right)):
        for part in range(quarter // HEAD):
            at = (2 * side + part) * LANES
            own[0:HEAD, at : at + LANES] = halo[part * HEAD : (part + 1) * HEAD, :]
    own[HEAD : HEAD + 8, :] = jnp.concatenate([about] * (columns // LANES), axis=1)
    own[HEAD + 8 :, :] = first_rows[...].astype(jnp.float32)
    wide_first[:, 0:columns] = first_rows[0:ROWHALO, :].astype(jnp.float32)
    wide_last[0:ROWHALO, 0:columns] = last_rows[...].astype(jnp.float32)
    for side, halo in enumerate((left, right)):
        at = columns + side * LANES
        wide_first[:, at : at + LANES] = halo[0:ROWHALO, :]
        wide_last[0:ROWHALO, at : at + LANES] = halo[quarter - ROWHALO : quarter, :]
    wide_last[ROWHALO:, :] = jnp.concatenate([about] * (columns // LANES + 2), axis=1)


def widen_kernel(begins, record, wait, *own):
    for begin, out in zip(begins, own):
        out[...] = record[begin : begin + out.shape[0], :].astype(jnp.float32)


def pass_on_kernel(unread, own, far, *refs):
    sent, sem = refs[unread], refs[-1]
    odd = lax.rem(lax.axis_index("shot"), 2) == 1
    pl.when(odd)(lambda: pltpu.make_async_copy(own, sent, sem).start())
    pl.when(jnp.logical_not(odd))(lambda: pltpu.make_async_copy(far, sent, sem).start())
    pltpu.make_async_copy(own, sent, sem).wait()


def shots_kernel(second_last, last, mine, following, second, out):
    lane = lax.broadcasted_iota(jnp.int32, (8, LANES), 1)
    row = lax.broadcasted_iota(jnp.int32, (8, LANES), 0)
    found = jnp.zeros((8, LANES), jnp.float32)
    for n, pair in enumerate((second_last, last, mine, following, second)):
        if n in (0, 2):
            value = jnp.where(lane == 0, pair[0], pair[1])
        else:
            value = pair[0:1, :]
        found = jnp.where(row == n, value, found)
    out[...] = found.astype(jnp.int32)


def on_device(record, offsets, lengths, thresholds):
    seg, columns = record.shape
    window = 2 * seg
    shots = lax.axis_size("shot")
    q = seg // QUARTERS
    skip = HEAD + 8
    parts = [0, 7 * seg // 64, 15 * seg // 32, 47 * seg // 64, seg]
    swap = [(i, i ^ 1) for i in range(shots) if i ^ 1 < shots]
    smem = pl.BlockSpec(memory_space=pltpu.SMEM)
    anywhere = pl.BlockSpec(memory_space=pl.ANY)
    vmem = pl.BlockSpec(memory_space=pltpu.VMEM)

    def array(*shape):
        return jax.ShapeDtypeStruct(shape, jnp.float32)

    def part(k):
        return array(parts[k + 1] - parts[k] + (skip if k == 0 else 0), columns)

    def window_of(rows, width, row, column):
        return pl.BlockSpec((rows, width), lambda _: (row, column))

    first_edge, last_edge = pl.pallas_call(
        prepare_kernel,
        grid=(1,),
        out_shape=(array(q, LANES), array(q, LANES)),
        in_specs=[window_of(seg, LANES, 0, 0), window_of(seg, LANES, 0, columns // LANES - 1)],
        out_specs=(vmem, vmem),
    )(record, record)
    from_left = shifted(last_edge, "rcv", 1)
    from_right = shifted(first_edge, "rcv", -1)
    mine = jnp.concatenate([offsets, lengths]).astype(jnp.float32)
    wide = columns + 2 * LANES
    first_part, wide_first, wide_last = pl.pallas_call(
        header_kernel,
        grid=(1,),
        out_shape=(part(0), array(ROWHALO, wide), array(ROWHALO + 8, wide)),
        in_specs=[smem, smem, window_of(parts[1], columns, 0, 0),
                  window_of(ROWHALO, columns, seg // ROWHALO - 1, 0), vmem, vmem],
        out_specs=(vmem,) * 3,
    )(offsets, lengths, record, record, from_left, from_right)
    swap = [(i, i ^ 1) for i in range(shots) if i ^ 1 < shots]
    far, near = [None] * 4, [None] * 4
    second_last = shifted(mine, "shot", 2)
    top = shifted(wide_last, "shot", 1)
    bot = shifted(wide_first, "shot", -3)
    far[0] = shifted(first_part, "shot", -2)
    own = [first_part] + list(pl.pallas_call(
        functools.partial(widen_kernel, parts[1:4]),
        out_shape=tuple(part(k) for k in (1, 2, 3)),
        in_specs=[vmem, anywhere],
        out_specs=(vmem,) * 3,
    )(record, top))
    far[1] = shifted(own[1], "shot", -2)

    def pass_on(k, *others):
        ahead = [own[k + 2]] if k + 2 < 4 else []
        sent, *ahead = pl.pallas_call(
            functools.partial(pass_on_kernel, len(ahead) + len(others)),
            out_shape=(part(k),) + tuple(array(*x.shape) for x in ahead),
            in_specs=[anywhere] * (2 + len(ahead) + len(others)),
            out_specs=(vmem,) + (anywhere,) * len(ahead),
            input_output_aliases={2: 1} if ahead else {},
            scratch_shapes=[pltpu.SemaphoreType.DMA],
        )(own[k], far[k], *ahead, *others)
        near[k] = lax.ppermute(sent, "shot", swap)
        if ahead:
            own[k + 2] = ahead[0]
            far[k + 2] = shifted(own[k + 2], "shot", -2)
        return sent

    pass_on(0)

    def corner(row):
        return pl.BlockSpec((8, LANES), lambda _: (row // 8, 0))

    params = pl.pallas_call(
        shots_kernel,
        grid=(1,),
        out_shape=jax.ShapeDtypeStruct((8, LANES), jnp.int32),
        in_specs=[smem, corner(ROWHALO), smem, corner(HEAD), corner(HEAD)],
        out_specs=vmem,
    )(second_last, top, mine, near[0], far[0])
    pass_on(1, params, bot)

    into, back = ring_matrices(columns)
    work = pltpu.VMEM((PLANES, window + 4 * PAD, LANES), jnp.float32)

    def phase(out, arrays, pieces, halo_places, outers, span):
        held = [] if out is None else [out]
        return pl.pallas_call(
            functools.partial(
                deblend_kernel, (seg, columns), pieces, halo_places, outers, span, 2 + len(arrays) + len(held)
            ),
            out_shape=array(1, window, columns),
            in_specs=[smem, smem] + [anywhere] * (2 + len(arrays) + len(held)),
            out_specs=anywhere,
            input_output_aliases={} if out is None else {4 + len(arrays): 0},
            scratch_shapes=[
                pltpu.VMEM(into.shape, into.dtype),
                pltpu.VMEM(back.shape, back.dtype),
                pltpu.VMEM((3 * seg, columns), jnp.float32),
                pltpu.VMEM((3, HEAD, columns), jnp.float32),
                pltpu.VMEM((2, ROWHALO, wide), jnp.float32),
                pltpu.VMEM((2, PLANES, 3 * seg + 4 * PAD, LANES), jnp.float32),
                work, work, work,
                pltpu.VMEM((3, PLANES, STRIP + 32, LANES), jnp.float32),
                pltpu.VMEM((window + BLOCK, columns), jnp.float32),
                pltpu.SemaphoreType.DMA((len(pieces) + 7,)),
                pltpu.SemaphoreType.DMA((window // BLOCK,)),
            ],
            compiler_params=pltpu.CompilerParams(vmem_limit_bytes=63 * 1024 * 1024),
        )(params, thresholds, into, back, *arrays, *held)

    def part_piece(k, main, segment):
        return (main, skip if k == 0 else 0, parts[k + 1] - parts[k], segment * seg + parts[k])

    blocks = window // BLOCK
    cap = 9

    def mark(offset, rows):
        return jnp.clip((seg + rows - 28 - offset) // BLOCK, 0, blocks)

    def far_begin(offset):
        return jnp.minimum((2 * seg + 35 - offset) // 8 * 8 // BLOCK, blocks)

    def far_middle(offset):
        return jnp.clip((2 * seg + parts[2] - 28 - offset) // BLOCK, far_begin(offset), blocks)

    def takes_far(offset):
        return far_middle(offset) - far_begin(offset) >= 4

    def first(offset):
        is_far = takes_far(offset)
        begin = jnp.where(is_far, far_begin(offset), 0)
        return [(begin, jnp.where(is_far, far_middle(offset), jnp.minimum(mark(offset, 0), cap)))]

    def second(offset):
        is_far = takes_far(offset)
        begin = jnp.where(is_far, 0, first(offset)[0][1])
        return [(begin, mark(offset, parts[2])), (jnp.where(is_far, far_middle(offset), far_begin(offset)), blocks)]

    def last(offset):
        bridged = (jnp.minimum((2 * seg + 35 - offset) // 8 * 8, window) + BLOCK - 1) // BLOCK
        return [(mark(offset, parts[2]), bridged)]

    def every(places, segment):
        return [part_piece(k, place, segment) for k, place in enumerate(places)]

    out = phase(
        None, [*own, top, far[0], far[1]], every(range(4), 0) + every((5, 6), 2), (0, None, 5), [(4, -ROWHALO)], first
    )
    pass_on(2, out)
    sent = pass_on(3)
    out = phase(
        out, [*far, *own, near[0], near[1], bot, top, sent],
        every(range(4), 2) + every(range(4, 8), 0) + every((8, 9), 1), (4, 8, 0),
        [(10, 3 * seg), (11, -ROWHALO)], second,
    )
    return phase(
        out, [own[0], own[3], *near, far[0], far[1]],
        [part_piece(3, 1, 0)] + every(range(2, 6), 1) + every((6, 7), 2), (0, 2, 6), [], last,
    )


def solution(mesh):
    return jax.shard_map(
        on_device,
        mesh=mesh,
        in_specs=(P("shot", "rcv"), P("shot"), P("shot"), P()),
        out_specs=P("shot", None, "rcv"),
        check_vma=False,
    )
```

```python
import functools

import numpy as np
import jax
import jax.numpy as jnp
from jax import lax
from jax.experimental import pallas as pl
from jax.experimental.pallas import tpu as pltpu
from jax.sharding import PartitionSpec as P

LEVELS = 3
relax_step = 0.5

PLANES = 5
LANES = 128
RING = PLANES * LANES
HALF = LANES // 2
EDGE = 32
QUARTERS = LANES // EDGE
HEAD = 128
PAD = 64
ROWHALO = 16
BLOCK = 64
STRIP = 64


def shifted(shard, axis, by):
    devices = lax.axis_size(axis)
    pairs = [(i, i + by) for i in range(devices) if 0 <= i + by < devices]
    return lax.ppermute(shard, axis, pairs)


def ring_matrices(columns):
    wide = columns + 2 * LANES
    into = np.zeros((wide, RING), np.float32)
    back = np.zeros((RING, columns), np.float32)

    def place(ring):
        pair, side = divmod(ring, 2)
        return (pair % PLANES) * LANES + side * HALF + pair // PLANES

    for column in range(columns):
        into[column, place(EDGE + column)] = relax_step
        back[place(EDGE + column), column] = 1.0
    for quarter in range(LANES // EDGE):
        for i in range(EDGE):
            into[columns + quarter * EDGE + i, place(i)] = relax_step
            into[columns + LANES + quarter * EDGE + i, place(EDGE + columns + i)] = relax_step
    return jnp.asarray(into, jnp.bfloat16), jnp.asarray(back, jnp.bfloat16)


def smooth_across(planes, dilation):
    if dilation == 1:
        lane = lax.broadcasted_iota(jnp.int32, planes[0].shape, 1)
        other = [pltpu.roll(x, HALF, 1) for x in planes]
        before = [pltpu.roll(planes[-1], HALF + 1, 1)] + other[:-1]
        after = other[1:] + [pltpu.roll(planes[0], HALF - 1, 1)]
        two_before = [pltpu.roll(planes[-1], 1, 1)] + planes[:-1]
        two_after = planes[1:] + [pltpu.roll(planes[0], LANES - 1, 1)]
        return [
            (two_before[k] + two_after[k])
            + 4.0 * (other[k] + jnp.where(lane < HALF, before[k], after[k]))
            + 6.0 * planes[k]
            for k in range(PLANES)
        ]
    rolled = {}
    pairs = dilation // 2

    def at(position):
        turns, plane = divmod(position, PLANES)
        if turns == 0:
            return planes[plane]
        if (turns, plane) not in rolled:
            rolled[turns, plane] = pltpu.roll(planes[plane], (-turns) % LANES, 1)
        return rolled[turns, plane]

    return [
        (at(k - 2 * pairs) + at(k + 2 * pairs)) + 4.0 * (at(k - pairs) + at(k + pairs)) + 6.0 * planes[k]
        for k in range(PLANES)
    ]


def limit(values, cut):
    return jnp.minimum(jnp.maximum(values, -cut), cut)


def blocks_of(first, count, body):
    def step(b, carry):
        body(pl.multiple_of(first + b * (2 * BLOCK), 8), 2 * BLOCK)
        return carry

    lax.fori_loop(0, count // 2, step, 0)
    pl.when(count % 2 == 1)(lambda: body(pl.multiple_of(first + (count - 1) * BLOCK, 8), BLOCK))


def smooth_block(ref, start, rows, dilation, scale):
    centre, summed = [], []
    for k in range(PLANES):
        x = [ref[k, pl.ds(start + tap * dilation, rows), :] for tap in range(-2, 3)]
        centre.append(x[2])
        summed.append((x[0] + x[4]) + 4.0 * (x[1] + x[3]) + 6.0 * x[2])
    summed = smooth_across(summed, dilation)
    return centre, [s * w for s, w in zip(summed, scale)]


def deblend_kernel(geometry, pieces, halo_places, outers, span, operands, params, thr, *refs):
    seg, columns = geometry
    into_hbm, back_hbm, *sources = refs[:operands]
    out, into, back, ext, halos, beyond, gathered, c1, c2, f, strip, staged, sem, out_sem = refs[operands:]
    window = 2 * seg
    quarter_rows = seg // QUARTERS

    shots = lax.axis_size("shot")
    me = lax.axis_index("shot")
    rcv = lax.axis_index("rcv")
    offset = params[2, 0]
    live = params[2, 1]
    total = (shots - me) * seg - offset

    def shot(by):
        return by * seg + params[by + 2, 0] - offset, params[by + 2, 1]

    live_blocks = (live + BLOCK - 1) // BLOCK
    whole = [(begin, jnp.maximum(end, begin)) for begin, end in span(offset)]
    spans = [
        (pl.multiple_of(begin * BLOCK, 8), jnp.maximum(jnp.minimum(end, live_blocks) - begin, 0)) for begin, end in whole
    ]
    some = sum(count for _, count in spans) > 0

    def reached(row, rows):
        found = False
        for low, count in spans:
            inside = (row < offset + low + count * BLOCK + 40) & (row + rows > offset + low - 40)
            found = found | ((count > 0) & inside)
        return found

    def copy_of(n, src, target):
        return pltpu.make_async_copy(src, target, sem.at[n])

    brought = [(0, None, into, some)]
    for main, first, rows, row in pieces:
        brought.append((main, (first, rows), ext.at[pl.ds(row, rows), :], reached(row, rows)))
    for segment, place in enumerate(halo_places):
        if place is not None:
            brought.append((place, (0, HEAD), halos.at[segment], some))
    for n, (place, row) in enumerate(outers):
        brought.append((place, (0, ROWHALO), beyond.at[n], reached(row, ROWHALO)))

    pl.when(some)(lambda: copy_of(0, into_hbm, into).start())
    for n, (place, part, target, wanted) in enumerate(brought):
        if part is not None:
            pl.when(wanted)(lambda: copy_of(n, sources[place].at[pl.ds(*part), :], target).start())
    pl.when(some)(lambda: copy_of(len(brought), back_hbm, back).start())

    lane = lax.broadcasted_iota(jnp.int32, (1, LANES), 1)
    has_right = jnp.where(rcv < lax.axis_size("rcv") - 1, 1.0, 0.0)
    has_left = jnp.where(rcv > 0, 1.0, 0.0)
    scale = []
    for k in range(PLANES):
        ring = 2 * (lane % HALF * PLANES + k) + lane // HALF
        side = jnp.where(ring < EDGE, has_left, has_right)
        scale.append(jnp.where((ring >= EDGE) & (ring < EDGE + columns), 1.0, side) * (1.0 / 256.0))
    strip[:, :, 0:16, :] = jnp.zeros((3, PLANES, 16, LANES), jnp.float32)
    strip[:, :, 16 + STRIP : 32 + STRIP, :] = jnp.zeros((3, PLANES, 16, LANES), jnp.float32)

    for n, (place, part, target, wanted) in enumerate(brought):
        pl.when(wanted)(lambda: copy_of(n, target, target).wait())

    def permute_in(main, left, right, quarter, row):
        mine = (lane // EDGE) == quarter
        lhs = [main] + [jnp.where(mine, x, 0.0) for x in (left, right)]
        lhs = jnp.concatenate([x.astype(jnp.bfloat16) for x in lhs], axis=1)
        result = jnp.dot(lhs, into[...], preferred_element_type=jnp.float32)
        for k in range(PLANES):
            gathered[0, k, pl.ds(PAD + row, main.shape[0]), :] = result[:, k * LANES : (k + 1) * LANES]

    def permute_quarter(i, carry):
        row = pl.multiple_of(i * quarter_rows, quarter_rows)
        segment = row // seg
        sides = []
        for side in range(2):
            lanes = [2 * side * LANES + at // HEAD * LANES for at in range(0, quarter_rows, HEAD)]
            sides.append(jnp.concatenate([halos[segment, :, at : at + LANES] for at in lanes], axis=0))
        permute_in(ext[pl.ds(row, quarter_rows), :], *sides, lax.rem(row, seg) // quarter_rows, row)
        return carry

    for low, count in spans:
        begin = jnp.clip((offset + low - 40) // quarter_rows, 0, 3 * QUARTERS)
        end = jnp.clip((offset + low + count * BLOCK + 40 + quarter_rows - 1) // quarter_rows, 0, 3 * QUARTERS)
        lax.fori_loop(begin, jnp.where(count > 0, end, begin), permute_quarter, 0)
    for n, (place, row) in enumerate(outers):

        @pl.when(reached(row, ROWHALO))
        def _():
            sides = [beyond[n, :, columns + side * LANES : columns + (side + 1) * LANES] for side in range(2)]
            permute_in(beyond[n, :, 0:columns], *sides, QUARTERS - 1 if row < 0 else 0, row)

    def level_pass(source, shift, target, dilation, first, count):
        def body(at, rows):
            _, summed = smooth_block(source, at + shift, rows, dilation, scale)
            for k in range(PLANES):
                target[k, pl.ds(at, rows), :] = summed[k]

        blocks_of(first, count, body)

    def shrunk(sweep, shift, at, rows):
        centre, summed = smooth_block(c2, at, rows, 4, scale)
        for k in range(PLANES):
            x0 = gathered[sweep, k, pl.ds(at + shift, rows), :]
            x1 = c1[k, pl.ds(at, rows), :]
            x2 = centre[k]
            clipped = limit(x0 - x1, thr[0]) + limit(x1 - x2, thr[1]) + limit(x2 - summed[k], thr[2])
            yield k, x0, x0 - clipped

    def next_gathered(at, rows):
        t = at - PAD + lax.broadcasted_iota(jnp.int32, (rows, LANES), 0)
        shots_live = jnp.zeros(t.shape, jnp.float32)
        for by in range(-2, 3):
            begin, length = shot(by)
            shots_live = shots_live + jnp.where((t >= begin) & (t < begin + length), 1.0, 0.0)
        own_live = jnp.where((t >= 0) & (t < live), 1.0, 0.0)
        inside = jnp.where(t < total, relax_step, 0.0)
        factor = own_live * (1.0 - inside * shots_live)
        for k, x0, value in shrunk(0, offset, at, rows):
            f[k, pl.ds(at, rows), :] = value
            gathered[1, k, pl.ds(at, rows), :] = own_live * x0 + factor * value

    half = STRIP // 2

    def do_strip(by, at_end):
        begin, length = shot(by)
        p = begin + jnp.where(at_end, length, 0)
        t = p - half + lax.broadcasted_iota(jnp.int32, (STRIP, LANES), 0)
        in_live = jnp.where((t >= begin) & (t < begin + length), 1.0, 0.0)
        in_window = jnp.where((t >= begin) & (t < begin + window), 1.0, 0.0)
        for k in range(PLANES):
            strip[0, k, 16 : 16 + STRIP, :] = gathered[0, k, pl.ds(PAD + offset + p - half, STRIP), :] * in_live
        for j in range(2):
            _, summed = smooth_block(strip.at[j], 16, STRIP, 2**j, scale)
            for k in range(PLANES):
                strip[j + 1, k, 16 : 16 + STRIP, :] = summed[k] * in_window
        mid = half
        _, summed = smooth_block(strip.at[2], mid, 32, 4, scale)
        t = p - 16 + lax.broadcasted_iota(jnp.int32, (32, LANES), 0)
        in_window = jnp.where((t >= begin) & (t < begin + window), 1.0, 0.0)
        near_edge = (t >= begin) & (t < begin + length) & (t >= p - 14) & (t < p + 14)
        own_live = (t >= 0) & (t < live)
        inside = jnp.where(t < total, -relax_step, 0.0)
        weight = jnp.where(near_edge & own_live, inside + jnp.where(by == 0, 1.0, 0.0), 0.0)
        for k in range(PLANES):
            x0 = strip[0, k, mid : mid + 32, :]
            x1 = strip[1, k, mid : mid + 32, :]
            x2 = strip[2, k, mid : mid + 32, :]
            x3 = summed[k] * in_window
            clipped = limit(x0 - x1, thr[0]) + limit(x1 - x2, thr[1]) + limit(x2 - x3, thr[2])
            where = pl.ds(PAD + p - 16, 32)
            gathered[1, k, where, :] = gathered[1, k, where, :] + weight * (x0 - clipped - f[k, where, :])

    def out_copy(block):
        rows = pl.ds(pl.multiple_of(block * BLOCK, BLOCK), BLOCK)
        return pltpu.make_async_copy(staged.at[rows, :], out.at[0, rows, :], out_sem.at[block])

    def estimate(at, rows):
        t = at - PAD + lax.broadcasted_iota(jnp.int32, (rows, LANES), 0)
        own_live = jnp.where(t < live, 1.0, 0.0)
        high, rest = [], []
        for k, _, value in shrunk(1, 0, at, rows):
            x = own_live * value
            h = x.astype(jnp.bfloat16)
            high.append(h)
            rest.append((x - h.astype(jnp.float32)).astype(jnp.bfloat16))
        both = jnp.concatenate([jnp.concatenate(high, axis=1), jnp.concatenate(rest, axis=1)], axis=0)
        result = jnp.dot(both, back[...], preferred_element_type=jnp.float32)
        staged[pl.ds(pl.multiple_of(at - PAD, 8), rows), :] = result[:rows] + result[rows:]
        for n in range(rows // BLOCK):
            out_copy((at - PAD) // BLOCK + n).start()

    def clear_edges(ref):
        ref[:, PAD - 16 : PAD, :] = jnp.zeros((PLANES, 16, LANES), jnp.float32)
        ref[:, PAD + window : PAD + window + 16, :] = jnp.zeros((PLANES, 16, LANES), jnp.float32)

    def process(low, count):
        high = low + count * BLOCK
        first = PAD + low
        wider, many = first - BLOCK // 2, count + 1

        def strip_step(i, carry):
            by, at_end = i // 2 - 2, i % 2 == 1
            begin, length = shot(by)
            p = begin + jnp.where(at_end, length, 0)
            begins_at = jnp.where(at_end, p - 14, p)
            bottom = jnp.maximum(low - 14, 0)
            top = jnp.minimum(high + 14, live)

            @pl.when((length > 0) & (begins_at + 14 > bottom) & (begins_at < top))
            def _():
                do_strip(by, at_end)

            return carry

        level_pass(gathered.at[0], offset, c1, 1, wider, many)
        level_pass(c1, 0, c2, 2, wider, many)
        blocks_of(wider, many, next_gathered)
        lax.fori_loop(1, 10, strip_step, 0)
        clear_edges(gathered.at[1])
        level_pass(gathered.at[1], 0, c1, 1, wider, many)
        clear_edges(c1)
        level_pass(c1, 0, c2, 2, wider, many)
        clear_edges(c2)
        blocks_of(first, count, estimate)

    pl.when(some)(lambda: copy_of(len(brought), back, back).wait())

    def span_step(i, carry):
        low, count = spans[0]
        if len(spans) > 1:
            low, count = jnp.where(i == 0, low, spans[1][0]), jnp.where(i == 0, count, spans[1][1])
        pl.when(count > 0)(lambda: process(pl.multiple_of(low, 8), count))
        return carry

    lax.fori_loop(0, len(spans), span_step, 0)

    def wait(i, carry):
        out_copy(i).wait()
        return carry

    def clear(i, carry):
        staged[pl.ds(pl.multiple_of(i * BLOCK, BLOCK), BLOCK), :] = jnp.zeros((BLOCK, columns), jnp.float32)
        out_copy(i).start()
        return carry

    for begin, end in whole:
        lax.fori_loop(jnp.maximum(begin, live_blocks), end, clear, 0)
    for begin, end in whole:
        lax.fori_loop(begin, end, wait, 0)


def prepare_kernel(first_columns, last_columns, first_edge, last_edge):
    quarter = first_edge.shape[0]
    lane = lax.broadcasted_iota(jnp.int32, (1, LANES), 1)
    for out, source, inner in ((first_edge, first_columns, 0), (last_edge, last_columns, LANES - EDGE)):
        packed = jnp.zeros((quarter, LANES), jnp.float32)
        for q in range(QUARTERS):
            rows = source[q * quarter : (q + 1) * quarter, :].astype(jnp.float32)
            turn = (q * EDGE - inner) % LANES
            packed = jnp.where(lane // EDGE == q, pltpu.roll(rows, turn, 1) if turn else rows, packed)
        out[...] = packed


def header_kernel(offsets, lengths, first_rows, last_rows, left, right, own, wide_first, wide_last):
    quarter = left.shape[0]
    columns = own.shape[1]
    lane = lax.broadcasted_iota(jnp.int32, (8, LANES), 1)
    about = jnp.where(lane == 0, offsets[0], jnp.where(lane == 1, lengths[0], 0)).astype(jnp.float32)
    for side, halo in enumerate((left, right)):
        for part in range(quarter // HEAD):
            at = (2 * side + part) * LANES
            own[0:HEAD, at : at + LANES] = halo[part * HEAD : (part + 1) * HEAD, :]
    own[HEAD : HEAD + 8, :] = jnp.concatenate([about] * (columns // LANES), axis=1)
    own[HEAD + 8 :, :] = first_rows[...].astype(jnp.float32)
    wide_first[:, 0:columns] = first_rows[0:ROWHALO, :].astype(jnp.float32)
    wide_last[0:ROWHALO, 0:columns] = last_rows[...].astype(jnp.float32)
    for side, halo in enumerate((left, right)):
        at = columns + side * LANES
        wide_first[:, at : at + LANES] = halo[0:ROWHALO, :]
        wide_last[0:ROWHALO, at : at + LANES] = halo[quarter - ROWHALO : quarter, :]
    wide_last[ROWHALO:, :] = jnp.concatenate([about] * (columns // LANES + 2), axis=1)


def widen_kernel(begins, record, wait, *own):
    for begin, out in zip(begins, own):
        out[...] = record[begin : begin + out.shape[0], :].astype(jnp.float32)


def pass_on_kernel(unread, own, far, *refs):
    sent, sem = refs[unread], refs[-1]
    odd = lax.rem(lax.axis_index("shot"), 2) == 1
    pl.when(odd)(lambda: pltpu.make_async_copy(own, sent, sem).start())
    pl.when(jnp.logical_not(odd))(lambda: pltpu.make_async_copy(far, sent, sem).start())
    pltpu.make_async_copy(own, sent, sem).wait()


def shots_kernel(second_last, last, mine, following, second, out):
    lane = lax.broadcasted_iota(jnp.int32, (8, LANES), 1)
    row = lax.broadcasted_iota(jnp.int32, (8, LANES), 0)
    found = jnp.zeros((8, LANES), jnp.float32)
    for n, pair in enumerate((second_last, last, mine, following, second)):
        if n in (0, 2):
            value = jnp.where(lane == 0, pair[0], pair[1])
        else:
            value = pair[0:1, :]
        found = jnp.where(row == n, value, found)
    out[...] = found.astype(jnp.int32)


def on_device(record, offsets, lengths, thresholds):
    seg, columns = record.shape
    window = 2 * seg
    shots = lax.axis_size("shot")
    q = seg // QUARTERS
    skip = HEAD + 8
    parts = [0, 7 * seg // 64, 15 * seg // 32, 47 * seg // 64, seg]
    swap = [(i, i ^ 1) for i in range(shots) if i ^ 1 < shots]
    smem = pl.BlockSpec(memory_space=pltpu.SMEM)
    anywhere = pl.BlockSpec(memory_space=pl.ANY)
    vmem = pl.BlockSpec(memory_space=pltpu.VMEM)

    def array(*shape):
        return jax.ShapeDtypeStruct(shape, jnp.float32)

    def part(k):
        return array(parts[k + 1] - parts[k] + (skip if k == 0 else 0), columns)

    def window_of(rows, width, row, column):
        return pl.BlockSpec((rows, width), lambda _: (row, column))

    first_edge, last_edge = pl.pallas_call(
        prepare_kernel,
        grid=(1,),
        out_shape=(array(q, LANES), array(q, LANES)),
        in_specs=[window_of(seg, LANES, 0, 0), window_of(seg, LANES, 0, columns // LANES - 1)],
        out_specs=(vmem, vmem),
    )(record, record)
    from_left = shifted(last_edge, "rcv", 1)
    from_right = shifted(first_edge, "rcv", -1)
    mine = jnp.concatenate([offsets, lengths]).astype(jnp.float32)
    wide = columns + 2 * LANES
    first_part, wide_first, wide_last = pl.pallas_call(
        header_kernel,
        grid=(1,),
        out_shape=(part(0), array(ROWHALO, wide), array(ROWHALO + 8, wide)),
        in_specs=[smem, smem, window_of(parts[1], columns, 0, 0),
                  window_of(ROWHALO, columns, seg // ROWHALO - 1, 0), vmem, vmem],
        out_specs=(vmem,) * 3,
    )(offsets, lengths, record, record, from_left, from_right)
    swap = [(i, i ^ 1) for i in range(shots) if i ^ 1 < shots]
    far, near = [None] * 4, [None] * 4
    second_last = shifted(mine, "shot", 2)
    top = shifted(wide_last, "shot", 1)
    bot = shifted(wide_first, "shot", -3)
    far[0] = shifted(first_part, "shot", -2)
    own = [first_part] + list(pl.pallas_call(
        functools.partial(widen_kernel, parts[1:4]),
        out_shape=tuple(part(k) for k in (1, 2, 3)),
        in_specs=[vmem, anywhere],
        out_specs=(vmem,) * 3,
    )(record, top))
    far[1] = shifted(own[1], "shot", -2)

    def pass_on(k, *others):
        ahead = [own[k + 2]] if k + 2 < 4 else []
        sent, *ahead = pl.pallas_call(
            functools.partial(pass_on_kernel, len(ahead) + len(others)),
            out_shape=(part(k),) + tuple(array(*x.shape) for x in ahead),
            in_specs=[anywhere] * (2 + len(ahead) + len(others)),
            out_specs=(vmem,) + (anywhere,) * len(ahead),
            input_output_aliases={2: 1} if ahead else {},
            scratch_shapes=[pltpu.SemaphoreType.DMA],
        )(own[k], far[k], *ahead, *others)
        near[k] = lax.ppermute(sent, "shot", swap)
        if ahead:
            own[k + 2] = ahead[0]
            far[k + 2] = shifted(own[k + 2], "shot", -2)
        return sent

    pass_on(0)

    def corner(row):
        return pl.BlockSpec((8, LANES), lambda _: (row // 8, 0))

    params = pl.pallas_call(
        shots_kernel,
        grid=(1,),
        out_shape=jax.ShapeDtypeStruct((8, LANES), jnp.int32),
        in_specs=[smem, corner(ROWHALO), smem, corner(HEAD), corner(HEAD)],
        out_specs=vmem,
    )(second_last, top, mine, near[0], far[0])
    pass_on(1, params, bot)

    into, back = ring_matrices(columns)
    work = pltpu.VMEM((PLANES, window + 4 * PAD, LANES), jnp.float32)

    def phase(out, arrays, pieces, halo_places, outers, span):
        held = [] if out is None else [out]
        return pl.pallas_call(
            functools.partial(
                deblend_kernel, (seg, columns), pieces, halo_places, outers, span, 2 + len(arrays) + len(held)
            ),
            out_shape=array(1, window, columns),
            in_specs=[smem, smem] + [anywhere] * (2 + len(arrays) + len(held)),
            out_specs=anywhere,
            input_output_aliases={} if out is None else {4 + len(arrays): 0},
            scratch_shapes=[
                pltpu.VMEM(into.shape, into.dtype),
                pltpu.VMEM(back.shape, back.dtype),
                pltpu.VMEM((3 * seg, columns), jnp.float32),
                pltpu.VMEM((3, HEAD, columns), jnp.float32),
                pltpu.VMEM((2, ROWHALO, wide), jnp.float32),
                pltpu.VMEM((2, PLANES, 3 * seg + 4 * PAD, LANES), jnp.float32),
                work, work, work,
                pltpu.VMEM((3, PLANES, STRIP + 32, LANES), jnp.float32),
                pltpu.VMEM((window + BLOCK, columns), jnp.float32),
                pltpu.SemaphoreType.DMA((len(pieces) + 7,)),
                pltpu.SemaphoreType.DMA((window // BLOCK,)),
            ],
            compiler_params=pltpu.CompilerParams(vmem_limit_bytes=63 * 1024 * 1024),
        )(params, thresholds, into, back, *arrays, *held)

    def part_piece(k, main, segment):
        return (main, skip if k == 0 else 0, parts[k + 1] - parts[k], segment * seg + parts[k])

    blocks = window // BLOCK
    cap = 9

    def mark(offset, rows):
        return jnp.clip((seg + rows - 28 - offset) // BLOCK, 0, blocks)

    def far_begin(offset):
        return jnp.minimum((2 * seg + 35 - offset) // 8 * 8 // BLOCK, blocks)

    def far_middle(offset):
        return jnp.clip((2 * seg + parts[2] - 28 - offset) // BLOCK, far_begin(offset), blocks)

    def takes_far(offset):
        return far_middle(offset) - far_begin(offset) >= 4

    def first(offset):
        is_far = takes_far(offset)
        begin = jnp.where(is_far, far_begin(offset), 0)
        return [(begin, jnp.where(is_far, far_middle(offset), jnp.minimum(mark(offset, 0), cap)))]

    def second(offset):
        is_far = takes_far(offset)
        begin = jnp.where(is_far, 0, first(offset)[0][1])
        return [(begin, mark(offset, parts[2])), (jnp.where(is_far, far_middle(offset), far_begin(offset)), blocks)]

    def last(offset):
        bridged = (jnp.minimum((2 * seg + 35 - offset) // 8 * 8, window) + BLOCK - 1) // BLOCK
        return [(mark(offset, parts[2]), bridged)]

    def every(places, segment):
        return [part_piece(k, place, segment) for k, place in enumerate(places)]

    out = phase(
        None, [*own, top, far[0], far[1]], every(range(4), 0) + every((5, 6), 2), (0, None, 5), [(4, -ROWHALO)], first
    )
    pass_on(2, out)
    sent = pass_on(3)
    out = phase(
        out, [*far, *own, near[0], near[1], bot, top, sent],
        every(range(4), 2) + every(range(4, 8), 0) + every((8, 9), 1), (4, 8, 0),
        [(10, 3 * seg), (11, -ROWHALO)], second,
    )
    return phase(
        out, [own[0], own[3], *near, far[0], far[1]],
        [part_piece(3, 1, 0)] + every(range(2, 6), 1) + every((6, 7), 2), (0, 2, 6), [], last,
    )


def solution(mesh):
    return jax.shard_map(
        on_device,
        mesh=mesh,
        in_specs=(P("shot", "rcv"), P("shot"), P("shot"), P()),
        out_specs=P("shot", None, "rcv"),
        check_vma=False,
    )
```

```python
import functools

import numpy as np
import jax
import jax.numpy as jnp
from jax import lax
from jax.experimental import pallas as pl
from jax.experimental.pallas import tpu as pltpu
from jax.sharding import PartitionSpec as P

LEVELS = 3
relax_step = 0.5

PLANES = 5
LANES = 128
RING = PLANES * LANES
HALF = LANES // 2
EDGE = 32
QUARTERS = LANES // EDGE
HEAD = 128
PAD = 64
ROWHALO = 16
BLOCK = 64
STRIP = 64


def shifted(shard, axis, by):
    devices = lax.axis_size(axis)
    pairs = [(i, i + by) for i in range(devices) if 0 <= i + by < devices]
    return lax.ppermute(shard, axis, pairs)


def ring_matrices(columns):
    wide = columns + 2 * LANES
    into = np.zeros((wide, RING), np.float32)
    back = np.zeros((RING, columns), np.float32)

    def place(ring):
        pair, side = divmod(ring, 2)
        return (pair % PLANES) * LANES + side * HALF + pair // PLANES

    for column in range(columns):
        into[column, place(EDGE + column)] = relax_step
        back[place(EDGE + column), column] = 1.0
    for quarter in range(LANES // EDGE):
        for i in range(EDGE):
            into[columns + quarter * EDGE + i, place(i)] = relax_step
            into[columns + LANES + quarter * EDGE + i, place(EDGE + columns + i)] = relax_step
    return jnp.asarray(into, jnp.bfloat16), jnp.asarray(back, jnp.bfloat16)


def smooth_across(planes, dilation):
    if dilation == 1:
        lane = lax.broadcasted_iota(jnp.int32, planes[0].shape, 1)
        other = [pltpu.roll(x, HALF, 1) for x in planes]
        before = [pltpu.roll(planes[-1], HALF + 1, 1)] + other[:-1]
        after = other[1:] + [pltpu.roll(planes[0], HALF - 1, 1)]
        two_before = [pltpu.roll(planes[-1], 1, 1)] + planes[:-1]
        two_after = planes[1:] + [pltpu.roll(planes[0], LANES - 1, 1)]
        return [
            (two_before[k] + two_after[k])
            + 4.0 * (other[k] + jnp.where(lane < HALF, before[k], after[k]))
            + 6.0 * planes[k]
            for k in range(PLANES)
        ]
    rolled = {}
    pairs = dilation // 2

    def at(position):
        turns, plane = divmod(position, PLANES)
        if turns == 0:
            return planes[plane]
        if (turns, plane) not in rolled:
            rolled[turns, plane] = pltpu.roll(planes[plane], (-turns) % LANES, 1)
        return rolled[turns, plane]

    return [
        (at(k - 2 * pairs) + at(k + 2 * pairs)) + 4.0 * (at(k - pairs) + at(k + pairs)) + 6.0 * planes[k]
        for k in range(PLANES)
    ]


def limit(values, cut):
    return jnp.minimum(jnp.maximum(values, -cut), cut)


def blocks_of(first, count, body):
    def step(b, carry):
        body(pl.multiple_of(first + b * (2 * BLOCK), 8), 2 * BLOCK)
        return carry

    lax.fori_loop(0, count // 2, step, 0)
    pl.when(count % 2 == 1)(lambda: body(pl.multiple_of(first + (count - 1) * BLOCK, 8), BLOCK))


def smooth_block(ref, start, rows, dilation, scale):
    centre, summed = [], []
    for k in range(PLANES):
        x = [ref[k, pl.ds(start + tap * dilation, rows), :] for tap in range(-2, 3)]
        centre.append(x[2])
        summed.append((x[0] + x[4]) + 4.0 * (x[1] + x[3]) + 6.0 * x[2])
    summed = smooth_across(summed, dilation)
    return centre, [s * w for s, w in zip(summed, scale)]


def deblend_kernel(geometry, pieces, halo_places, outers, span, operands, params, thr, *refs):
    seg, columns = geometry
    into_hbm, back_hbm, *sources = refs[:operands]
    out, into, back, ext, halos, beyond, gathered, c1, c2, f, strip, staged, sem, out_sem = refs[operands:]
    window = 2 * seg
    quarter_rows = seg // QUARTERS

    shots = lax.axis_size("shot")
    me = lax.axis_index("shot")
    rcv = lax.axis_index("rcv")
    offset = params[2, 0]
    live = params[2, 1]
    total = (shots - me) * seg - offset

    def shot(by):
        return by * seg + params[by + 2, 0] - offset, params[by + 2, 1]

    live_blocks = (live + BLOCK - 1) // BLOCK
    whole = [(begin, jnp.maximum(end, begin)) for begin, end in span(offset)]
    spans = [
        (pl.multiple_of(begin * BLOCK, 8), jnp.maximum(jnp.minimum(end, live_blocks) - begin, 0)) for begin, end in whole
    ]
    some = sum(count for _, count in spans) > 0

    def reached(row, rows):
        found = False
        for low, count in spans:
            inside = (row < offset + low + count * BLOCK + 40) & (row + rows > offset + low - 40)
            found = found | ((count > 0) & inside)
        return found

    def copy_of(n, src, target):
        return pltpu.make_async_copy(src, target, sem.at[n])

    brought = [(0, None, into, some)]
    for main, first, rows, row in pieces:
        brought.append((main, (first, rows), ext.at[pl.ds(row, rows), :], reached(row, rows)))
    for segment, place in enumerate(halo_places):
        if place is not None:
            brought.append((place, (0, HEAD), halos.at[segment], some))
    for n, (place, row) in enumerate(outers):
        brought.append((place, (0, ROWHALO), beyond.at[n], reached(row, ROWHALO)))

    pl.when(some)(lambda: copy_of(0, into_hbm, into).start())
    for n, (place, part, target, wanted) in enumerate(brought):
        if part is not None:
            pl.when(wanted)(lambda: copy_of(n, sources[place].at[pl.ds(*part), :], target).start())
    pl.when(some)(lambda: copy_of(len(brought), back_hbm, back).start())

    lane = lax.broadcasted_iota(jnp.int32, (1, LANES), 1)
    has_right = jnp.where(rcv < lax.axis_size("rcv") - 1, 1.0, 0.0)
    has_left = jnp.where(rcv > 0, 1.0, 0.0)
    scale = []
    for k in range(PLANES):
        ring = 2 * (lane % HALF * PLANES + k) + lane // HALF
        side = jnp.where(ring < EDGE, has_left, has_right)
        scale.append(jnp.where((ring >= EDGE) & (ring < EDGE + columns), 1.0, side) * (1.0 / 256.0))
    strip[:, :, 0:16, :] = jnp.zeros((3, PLANES, 16, LANES), jnp.float32)
    strip[:, :, 16 + STRIP : 32 + STRIP, :] = jnp.zeros((3, PLANES, 16, LANES), jnp.float32)

    for n, (place, part, target, wanted) in enumerate(brought):
        pl.when(wanted)(lambda: copy_of(n, target, target).wait())

    def permute_in(main, left, right, quarter, row):
        mine = (lane // EDGE) == quarter
        lhs = [main] + [jnp.where(mine, x, 0.0) for x in (left, right)]
        lhs = jnp.concatenate([x.astype(jnp.bfloat16) for x in lhs], axis=1)
        result = jnp.dot(lhs, into[...], preferred_element_type=jnp.float32)
        for k in range(PLANES):
            gathered[0, k, pl.ds(PAD + row, main.shape[0]), :] = result[:, k * LANES : (k + 1) * LANES]

    def permute_quarter(i, carry):
        row = pl.multiple_of(i * quarter_rows, quarter_rows)
        segment = row // seg
        sides = []
        for side in range(2):
            lanes = [2 * side * LANES + at // HEAD * LANES for at in range(0, quarter_rows, HEAD)]
            sides.append(jnp.concatenate([halos[segment, :, at : at + LANES] for at in lanes], axis=0))
        permute_in(ext[pl.ds(row, quarter_rows), :], *sides, lax.rem(row, seg) // quarter_rows, row)
        return carry

    for low, count in spans:
        begin = jnp.clip((offset + low - 40) // quarter_rows, 0, 3 * QUARTERS)
        end = jnp.clip((offset + low + count * BLOCK + 40 + quarter_rows - 1) // quarter_rows, 0, 3 * QUARTERS)
        lax.fori_loop(begin, jnp.where(count > 0, end, begin), permute_quarter, 0)
    for n, (place, row) in enumerate(outers):

        @pl.when(reached(row, ROWHALO))
        def _():
            sides = [beyond[n, :, columns + side * LANES : columns + (side + 1) * LANES] for side in range(2)]
            permute_in(beyond[n, :, 0:columns], *sides, QUARTERS - 1 if row < 0 else 0, row)

    def level_pass(source, shift, target, dilation, first, count):
        def body(at, rows):
            _, summed = smooth_block(source, at + shift, rows, dilation, scale)
            for k in range(PLANES):
                target[k, pl.ds(at, rows), :] = summed[k]

        blocks_of(first, count, body)

    def shrunk(sweep, shift, at, rows):
        centre, summed = smooth_block(c2, at, rows, 4, scale)
        for k in range(PLANES):
            x0 = gathered[sweep, k, pl.ds(at + shift, rows), :]
            x1 = c1[k, pl.ds(at, rows), :]
            x2 = centre[k]
            clipped = limit(x0 - x1, thr[0]) + limit(x1 - x2, thr[1]) + limit(x2 - summed[k], thr[2])
            yield k, x0, x0 - clipped

    def next_gathered(at, rows):
        t = at - PAD + lax.broadcasted_iota(jnp.int32, (rows, LANES), 0)
        shots_live = jnp.zeros(t.shape, jnp.float32)
        for by in range(-2, 3):
            begin, length = shot(by)
            shots_live = shots_live + jnp.where((t >= begin) & (t < begin + length), 1.0, 0.0)
        own_live = jnp.where((t >= 0) & (t < live), 1.0, 0.0)
        inside = jnp.where(t < total, relax_step, 0.0)
        factor = own_live * (1.0 - inside * shots_live)
        for k, x0, value in shrunk(0, offset, at, rows):
            f[k, pl.ds(at, rows), :] = value
            gathered[1, k, pl.ds(at, rows), :] = own_live * x0 + factor * value

    half = STRIP // 2

    def do_strip(by, at_end):
        begin, length = shot(by)
        p = begin + jnp.where(at_end, length, 0)
        t = p - half + lax.broadcasted_iota(jnp.int32, (STRIP, LANES), 0)
        in_live = jnp.where((t >= begin) & (t < begin + length), 1.0, 0.0)
        in_window = jnp.where((t >= begin) & (t < begin + window), 1.0, 0.0)
        for k in range(PLANES):
            strip[0, k, 16 : 16 + STRIP, :] = gathered[0, k, pl.ds(PAD + offset + p - half, STRIP), :] * in_live
        for j in range(2):
            _, summed = smooth_block(strip.at[j], 16, STRIP, 2**j, scale)
            for k in range(PLANES):
                strip[j + 1, k, 16 : 16 + STRIP, :] = summed[k] * in_window
        mid = half
        _, summed = smooth_block(strip.at[2], mid, 32, 4, scale)
        t = p - 16 + lax.broadcasted_iota(jnp.int32, (32, LANES), 0)
        in_window = jnp.where((t >= begin) & (t < begin + window), 1.0, 0.0)
        near_edge = (t >= begin) & (t < begin + length) & (t >= p - 14) & (t < p + 14)
        own_live = (t >= 0) & (t < live)
        inside = jnp.where(t < total, -relax_step, 0.0)
        weight = jnp.where(near_edge & own_live, inside + jnp.where(by == 0, 1.0, 0.0), 0.0)
        for k in range(PLANES):
            x0 = strip[0, k, mid : mid + 32, :]
            x1 = strip[1, k, mid : mid + 32, :]
            x2 = strip[2, k, mid : mid + 32, :]
            x3 = summed[k] * in_window
            clipped = limit(x0 - x1, thr[0]) + limit(x1 - x2, thr[1]) + limit(x2 - x3, thr[2])
            where = pl.ds(PAD + p - 16, 32)
            gathered[1, k, where, :] = gathered[1, k, where, :] + weight * (x0 - clipped - f[k, where, :])

    def out_copy(block):
        rows = pl.ds(pl.multiple_of(block * BLOCK, BLOCK), BLOCK)
        return pltpu.make_async_copy(staged.at[rows, :], out.at[0, rows, :], out_sem.at[block])

    def estimate(at, rows):
        t = at - PAD + lax.broadcasted_iota(jnp.int32, (rows, LANES), 0)
        own_live = jnp.where(t < live, 1.0, 0.0)
        high, rest = [], []
        for k, _, value in shrunk(1, 0, at, rows):
            x = own_live * value
            h = x.astype(jnp.bfloat16)
            high.append(h)
            rest.append((x - h.astype(jnp.float32)).astype(jnp.bfloat16))
        both = jnp.concatenate([jnp.concatenate(high, axis=1), jnp.concatenate(rest, axis=1)], axis=0)
        result = jnp.dot(both, back[...], preferred_element_type=jnp.float32)
        staged[pl.ds(pl.multiple_of(at - PAD, 8), rows), :] = result[:rows] + result[rows:]
        for n in range(rows // BLOCK):
            out_copy((at - PAD) // BLOCK + n).start()

    def clear_edges(ref):
        ref[:, PAD - 16 : PAD, :] = jnp.zeros((PLANES, 16, LANES), jnp.float32)
        ref[:, PAD + window : PAD + window + 16, :] = jnp.zeros((PLANES, 16, LANES), jnp.float32)

    def process(low, count):
        high = low + count * BLOCK
        first = PAD + low
        wider, many = first - BLOCK // 2, count + 1

        def strip_step(i, carry):
            by, at_end = i // 2 - 2, i % 2 == 1
            begin, length = shot(by)
            p = begin + jnp.where(at_end, length, 0)
            begins_at = jnp.where(at_end, p - 14, p)
            bottom = jnp.maximum(low - 14, 0)
            top = jnp.minimum(high + 14, live)

            @pl.when((length > 0) & (begins_at + 14 > bottom) & (begins_at < top))
            def _():
                do_strip(by, at_end)

            return carry

        level_pass(gathered.at[0], offset, c1, 1, wider, many)
        level_pass(c1, 0, c2, 2, wider, many)
        blocks_of(wider, many, next_gathered)
        lax.fori_loop(1, 10, strip_step, 0)
        clear_edges(gathered.at[1])
        level_pass(gathered.at[1], 0, c1, 1, wider, many)
        clear_edges(c1)
        level_pass(c1, 0, c2, 2, wider, many)
        clear_edges(c2)
        blocks_of(first, count, estimate)

    pl.when(some)(lambda: copy_of(len(brought), back, back).wait())

    def span_step(i, carry):
        low, count = spans[0]
        if len(spans) > 1:
            low, count = jnp.where(i == 0, low, spans[1][0]), jnp.where(i == 0, count, spans[1][1])
        pl.when(count > 0)(lambda: process(pl.multiple_of(low, 8), count))
        return carry

    def clear(i, carry):
        staged[pl.ds(pl.multiple_of(i * BLOCK, BLOCK), BLOCK), :] = jnp.zeros((BLOCK, columns), jnp.float32)
        out_copy(i).start()
        return carry

    for begin, end in whole:
        lax.fori_loop(jnp.maximum(begin, live_blocks), end, clear, 0)
    lax.fori_loop(0, len(spans), span_step, 0)

    def wait(i, carry):
        out_copy(i).wait()
        return carry

    for begin, end in whole:
        lax.fori_loop(begin, end, wait, 0)


def prepare_kernel(first_columns, last_columns, first_edge, last_edge):
    quarter = first_edge.shape[0]
    lane = lax.broadcasted_iota(jnp.int32, (1, LANES), 1)
    for out, source, inner in ((first_edge, first_columns, 0), (last_edge, last_columns, LANES - EDGE)):
        packed = jnp.zeros((quarter, LANES), jnp.float32)
        for q in range(QUARTERS):
            rows = source[q * quarter : (q + 1) * quarter, :].astype(jnp.float32)
            turn = (q * EDGE - inner) % LANES
            packed = jnp.where(lane // EDGE == q, pltpu.roll(rows, turn, 1) if turn else rows, packed)
        out[...] = packed


def header_kernel(offsets, lengths, first_rows, last_rows, left, right, own, wide_first, wide_last):
    quarter = left.shape[0]
    columns = own.shape[1]
    lane = lax.broadcasted_iota(jnp.int32, (8, LANES), 1)
    about = jnp.where(lane == 0, offsets[0], jnp.where(lane == 1, lengths[0], 0)).astype(jnp.float32)
    for side, halo in enumerate((left, right)):
        for part in range(quarter // HEAD):
            at = (2 * side + part) * LANES
            own[0:HEAD, at : at + LANES] = halo[part * HEAD : (part + 1) * HEAD, :]
    own[HEAD : HEAD + 8, :] = jnp.concatenate([about] * (columns // LANES), axis=1)
    own[HEAD + 8 :, :] = first_rows[...].astype(jnp.float32)
    wide_first[:, 0:columns] = first_rows[0:ROWHALO, :].astype(jnp.float32)
    wide_last[0:ROWHALO, 0:columns] = last_rows[...].astype(jnp.float32)
    for side, halo in enumerate((left, right)):
        at = columns + side * LANES
        wide_first[:, at : at + LANES] = halo[0:ROWHALO, :]
        wide_last[0:ROWHALO, at : at + LANES] = halo[quarter - ROWHALO : quarter, :]
    wide_last[ROWHALO:, :] = jnp.concatenate([about] * (columns // LANES + 2), axis=1)


def widen_kernel(begins, record, wait, *own):
    for begin, out in zip(begins, own):
        out[...] = record[begin : begin + out.shape[0], :].astype(jnp.float32)


def pass_on_kernel(unread, own, far, *refs):
    sent, sem = refs[unread], refs[-1]
    odd = lax.rem(lax.axis_index("shot"), 2) == 1
    pl.when(odd)(lambda: pltpu.make_async_copy(own, sent, sem).start())
    pl.when(jnp.logical_not(odd))(lambda: pltpu.make_async_copy(far, sent, sem).start())
    pltpu.make_async_copy(own, sent, sem).wait()


def shots_kernel(second_last, last, mine, following, second, out):
    lane = lax.broadcasted_iota(jnp.int32, (8, LANES), 1)
    row = lax.broadcasted_iota(jnp.int32, (8, LANES), 0)
    found = jnp.zeros((8, LANES), jnp.float32)
    for n, pair in enumerate((second_last, last, mine, following, second)):
        if n in (0, 2):
            value = jnp.where(lane == 0, pair[0], pair[1])
        else:
            value = pair[0:1, :]
        found = jnp.where(row == n, value, found)
    out[...] = found.astype(jnp.int32)


def on_device(record, offsets, lengths, thresholds):
    seg, columns = record.shape
    window = 2 * seg
    shots = lax.axis_size("shot")
    q = seg // QUARTERS
    skip = HEAD + 8
    parts = [0, 7 * seg // 64, 15 * seg // 32, 47 * seg // 64, seg]
    swap = [(i, i ^ 1) for i in range(shots) if i ^ 1 < shots]
    smem = pl.BlockSpec(memory_space=pltpu.SMEM)
    anywhere = pl.BlockSpec(memory_space=pl.ANY)
    vmem = pl.BlockSpec(memory_space=pltpu.VMEM)

    def array(*shape):
        return jax.ShapeDtypeStruct(shape, jnp.float32)

    def part(k):
        return array(parts[k + 1] - parts[k] + (skip if k == 0 else 0), columns)

    def window_of(rows, width, row, column):
        return pl.BlockSpec((rows, width), lambda _: (row, column))

    first_edge, last_edge = pl.pallas_call(
        prepare_kernel,
        grid=(1,),
        out_shape=(array(q, LANES), array(q, LANES)),
        in_specs=[window_of(seg, LANES, 0, 0), window_of(seg, LANES, 0, columns // LANES - 1)],
        out_specs=(vmem, vmem),
    )(record, record)
    from_left = shifted(last_edge, "rcv", 1)
    from_right = shifted(first_edge, "rcv", -1)
    mine = jnp.concatenate([offsets, lengths]).astype(jnp.float32)
    wide = columns + 2 * LANES
    first_part, wide_first, wide_last = pl.pallas_call(
        header_kernel,
        grid=(1,),
        out_shape=(part(0), array(ROWHALO, wide), array(ROWHALO + 8, wide)),
        in_specs=[smem, smem, window_of(parts[1], columns, 0, 0),
                  window_of(ROWHALO, columns, seg // ROWHALO - 1, 0), vmem, vmem],
        out_specs=(vmem,) * 3,
    )(offsets, lengths, record, record, from_left, from_right)
    swap = [(i, i ^ 1) for i in range(shots) if i ^ 1 < shots]
    far, near = [None] * 4, [None] * 4
    second_last = shifted(mine, "shot", 2)
    top = shifted(wide_last, "shot", 1)
    bot = shifted(wide_first, "shot", -3)
    far[0] = shifted(first_part, "shot", -2)
    own = [first_part] + list(pl.pallas_call(
        functools.partial(widen_kernel, parts[1:4]),
        out_shape=tuple(part(k) for k in (1, 2, 3)),
        in_specs=[vmem, anywhere],
        out_specs=(vmem,) * 3,
    )(record, top))
    far[1] = shifted(own[1], "shot", -2)

    def pass_on(k, *others):
        ahead = [own[k + 2]] if k + 2 < 4 else []
        sent, *ahead = pl.pallas_call(
            functools.partial(pass_on_kernel, len(ahead) + len(others)),
            out_shape=(part(k),) + tuple(array(*x.shape) for x in ahead),
            in_specs=[anywhere] * (2 + len(ahead) + len(others)),
            out_specs=(vmem,) + (anywhere,) * len(ahead),
            input_output_aliases={2: 1} if ahead else {},
            scratch_shapes=[pltpu.SemaphoreType.DMA],
        )(own[k], far[k], *ahead, *others)
        near[k] = lax.ppermute(sent, "shot", swap)
        if ahead:
            own[k + 2] = ahead[0]
            far[k + 2] = shifted(own[k + 2], "shot", -2)
        return sent

    pass_on(0)

    def corner(row):
        return pl.BlockSpec((8, LANES), lambda _: (row // 8, 0))

    params = pl.pallas_call(
        shots_kernel,
        grid=(1,),
        out_shape=jax.ShapeDtypeStruct((8, LANES), jnp.int32),
        in_specs=[smem, corner(ROWHALO), smem, corner(HEAD), corner(HEAD)],
        out_specs=vmem,
    )(second_last, top, mine, near[0], far[0])
    pass_on(1, params, bot)

    into, back = ring_matrices(columns)
    work = pltpu.VMEM((PLANES, window + 4 * PAD, LANES), jnp.float32)

    def phase(out, arrays, pieces, halo_places, outers, span):
        held = [] if out is None else [out]
        return pl.pallas_call(
            functools.partial(
                deblend_kernel, (seg, columns), pieces, halo_places, outers, span, 2 + len(arrays) + len(held)
            ),
            out_shape=array(1, window, columns),
            in_specs=[smem, smem] + [anywhere] * (2 + len(arrays) + len(held)),
            out_specs=anywhere,
            input_output_aliases={} if out is None else {4 + len(arrays): 0},
            scratch_shapes=[
                pltpu.VMEM(into.shape, into.dtype),
                pltpu.VMEM(back.shape, back.dtype),
                pltpu.VMEM((3 * seg, columns), jnp.float32),
                pltpu.VMEM((3, HEAD, columns), jnp.float32),
                pltpu.VMEM((2, ROWHALO, wide), jnp.float32),
                pltpu.VMEM((2, PLANES, 3 * seg + 4 * PAD, LANES), jnp.float32),
                work, work, work,
                pltpu.VMEM((3, PLANES, STRIP + 32, LANES), jnp.float32),
                pltpu.VMEM((window + BLOCK, columns), jnp.float32),
                pltpu.SemaphoreType.DMA((len(pieces) + 7,)),
                pltpu.SemaphoreType.DMA((window // BLOCK,)),
            ],
            compiler_params=pltpu.CompilerParams(vmem_limit_bytes=63 * 1024 * 1024),
        )(params, thresholds, into, back, *arrays, *held)

    def part_piece(k, main, segment):
        return (main, skip if k == 0 else 0, parts[k + 1] - parts[k], segment * seg + parts[k])

    blocks = window // BLOCK
    cap = 9

    def mark(offset, rows):
        return jnp.clip((seg + rows - 28 - offset) // BLOCK, 0, blocks)

    def far_begin(offset):
        return jnp.minimum((2 * seg + 35 - offset) // 8 * 8 // BLOCK, blocks)

    def far_middle(offset):
        return jnp.clip((2 * seg + parts[2] - 28 - offset) // BLOCK, far_begin(offset), blocks)

    def takes_far(offset):
        return far_middle(offset) - far_begin(offset) >= 4

    def first(offset):
        is_far = takes_far(offset)
        begin = jnp.where(is_far, far_begin(offset), 0)
        return [(begin, jnp.where(is_far, far_middle(offset), jnp.minimum(mark(offset, 0), cap)))]

    def second(offset):
        is_far = takes_far(offset)
        begin = jnp.where(is_far, 0, first(offset)[0][1])
        return [(begin, mark(offset, parts[2])), (jnp.where(is_far, far_middle(offset), far_begin(offset)), blocks)]

    def last(offset):
        bridged = (jnp.minimum((2 * seg + 35 - offset) // 8 * 8, window) + BLOCK - 1) // BLOCK
        return [(mark(offset, parts[2]), bridged)]

    def every(places, segment):
        return [part_piece(k, place, segment) for k, place in enumerate(places)]

    out = phase(
        None, [*own, top, far[0], far[1]], every(range(4), 0) + every((5, 6), 2), (0, None, 5), [(4, -ROWHALO)], first
    )
    pass_on(2, out)
    sent = pass_on(3)
    out = phase(
        out, [*far, *own, near[0], near[1], bot, top, sent],
        every(range(4), 2) + every(range(4, 8), 0) + every((8, 9), 1), (4, 8, 0),
        [(10, 3 * seg), (11, -ROWHALO)], second,
    )
    return phase(
        out, [own[0], own[3], *near, far[0], far[1]],
        [part_piece(3, 1, 0)] + every(range(2, 6), 1) + every((6, 7), 2), (0, 2, 6), [], last,
    )


def solution(mesh):
    return jax.shard_map(
        on_device,
        mesh=mesh,
        in_specs=(P("shot", "rcv"), P("shot"), P("shot"), P()),
        out_specs=P("shot", None, "rcv"),
        check_vma=False,
    )
```
